512 devices in a mesh: row: 64 (over z_hi, x, y, core), col: 8 (over z_lo).
Axes of the slice: x: 4, y: 4, z: 16 (z_hi: 2, z_lo: 8; z = z_hi * 8 + z_lo), core: 2. Of those that a mesh axis runs over, the one named last changes fastest.
Arguments:
- density: bfloat16 [1024, 64, 1024], P('row', None, 'col'), may hold values from -0.9 to 1.9
- columns: int32 [1024, 16], replicated, may hold values from 0 to 1023, as said below
Outputs:
- purified: float32 [1024, 64, 1024], P('row', None, 'col')
The draws below stay inside these ranges and needn't reach their ends.
Inputs may be any that keep to these rules, and one draw needn't show every extreme that they name: Stored block a of row i lies in group a // 2: columns[i, a] is congruent to a // 2 modulo 8. The columns of a row are distinct and lie within cyclic distance 48 of i; row 0 always stores a block at distance exactly 48, and other rows may as well. The diagonal column i stands in slot (i mod 8) * 2.
All inputs are finite; a program needn't handle non-finite values.
Results may differ from the reference program's by a relative error of at most 0.0034.
Values may be sent and summed in bfloat16 or wider, within the bound.
No kernel may reach another device: no remote copies, remote signals or barrier semaphores. Data moves between devices by JAX's collectives and lax.ppermute only.
A program may use at most 64 MiB of HBM per device.

```python
import jax
import jax.numpy as jnp
from jax import lax

B = 64
K = 16
R_DEV = 16
NB = 1024
H = 48
GROUPS = 8
K_G = 2


def draw_columns(key, part):
    key = jax.random.fold_in(key, 11)
    count = (2 * H + 1) // GROUPS
    rows = jnp.arange(NB, dtype=jnp.int32)[:, None, None]
    groups = jnp.arange(GROUPS, dtype=jnp.int32)[None, :, None]
    steps = jnp.arange(count, dtype=jnp.int32)[None, None, :]
    first = jnp.mod(groups - rows + H, GROUPS) - H
    offsets = first + steps * GROUPS
    scores = jax.random.randint(key, (NB, GROUPS, count), 0, 1 << 20, dtype=jnp.int32) * count + steps
    scores = jnp.where(offsets == 0, -2, scores)
    scores = jnp.where((rows == 0) & (offsets == -H), -1, scores)
    order = jnp.argsort(scores, axis=-1)[..., :K_G]
    picked = jnp.take_along_axis(offsets, order, axis=-1)
    return jnp.mod(rows + picked, NB).reshape(NB, K).astype(jnp.int32)


def draw_density(key, part):
    key = jax.random.fold_in(key, 23)
    noise_key, fill_key = jax.random.split(key)
    noise = jnp.clip(0.15 * jax.random.normal(noise_key, (NB, B, K * B), jnp.float32), -0.9, 0.9)
    occupation = jax.random.uniform(fill_key, (NB, B, 1), jnp.float32, 0.0, 1.0)
    rows = jnp.arange(NB, dtype=jnp.int32)[:, None, None]
    line = jnp.arange(B, dtype=jnp.int32)[None, :, None]
    column = jnp.arange(K * B, dtype=jnp.int32)[None, None, :]
    target = jnp.mod(rows, GROUPS) * K_G * B + line
    return (noise + jnp.where(column == target, occupation, 0.0)).astype(jnp.bfloat16)


def setup_inputs(seed: int = 0) -> dict:
    streams_of = jax.random.split(jax.random.key(seed), 3)
    return {
        "density": draw_density(jax.random.fold_in(streams_of[2], 71), 0),
        "columns": draw_columns(jax.random.fold_in(streams_of[2], 71), 0),
    }


def to_blocks(values, count, width):
    return values.reshape(values.shape[0], width, count, width).transpose(0, 2, 1, 3)


def product(left, right, columns):
    count = columns.shape[1]
    width = left.shape[1]
    total = columns.shape[0]
    left_blocks = to_blocks(left, count, width).astype(jnp.float32)
    right_blocks = to_blocks(right, count, width).astype(jnp.float32)
    candidates = columns[columns]
    equal = candidates[:, None, :, :] == columns[:, :, None, None]
    live = jnp.any(equal, axis=-1)
    slots = jnp.arange(count, dtype=jnp.int32)
    chosen_slot = jnp.sum(jnp.where(equal, slots, 0), axis=-1).astype(jnp.int32)
    batches = total // R_DEV

    def one_batch(pieces):
        left_part, inner_rows, slot_part, live_part = pieces
        taken = right_blocks[inner_rows[:, None, :], slot_part]
        taken = jnp.where(live_part[..., None, None], taken, 0.0)
        return jnp.einsum("ibxy,iabyz->iaxz", left_part, taken)

    result = lax.map(one_batch, (left_blocks.reshape(batches, R_DEV, count, width, width),
                                 columns.reshape(batches, R_DEV, count),
                                 chosen_slot.reshape(batches, R_DEV, count, count),
                                 live.reshape(batches, R_DEV, count, count)))
    result = result.reshape(total, count, width, width)
    return result.transpose(0, 2, 1, 3).reshape(total, width, count * width)


def reference(density, columns):
    square = product(density, density, columns).astype(jnp.bfloat16)
    cube = product(square, density, columns)
    return 3.0 * square.astype(jnp.float32) - 2.0 * cube
```

```python
import jax
import jax.numpy as jnp
from jax import lax
from jax.experimental import pallas as pl
from jax.experimental.pallas import tpu as pltpu
from jax.sharding import PartitionSpec as P

PARTS = 2


def ring_order(count):
    return list(range(0, count, 2)) + list(range(count - 1, 0, -2))


def product_kernel(count, group, keep, index_ref, mask_ref, table_ref, *refs):
    chunks = refs[:count]
    out_ref = refs[-1]
    rows, width, lanes = chunks[0].shape
    blocks = count * group
    for i in range(rows):
        total = None
        for step in range(0, count, 2):
            left = jnp.concatenate([chunks[step][i], chunks[step + 1][i]], axis=1)
            pieces = []
            for b in range(step * group, (step + 2) * group):
                piece = table_ref[index_ref[i * blocks + b]]
                piece = jnp.concatenate([piece, piece], axis=1)
                mask = mask_ref[pl.ds(i * blocks + b, 1), :].astype(piece.dtype)
                pieces.append(piece * mask)
            right = jnp.concatenate(pieces, axis=0)
            part = jnp.dot(left, right, preferred_element_type=jnp.float32)
            total = part if total is None else total + part
        value = total[:, :lanes] + pltpu.roll(total[:, lanes:], width, 1)
        if keep:
            value = 3.0 * refs[count][i].astype(jnp.float32) - 2.0 * value
        out_ref[i] = value.astype(out_ref.dtype)


def product(index, mask, table, chunks, square=None):
    count = len(chunks)
    rows, width, lanes = chunks[0].shape
    group = lanes // width
    keep = square is not None
    vmem = pl.BlockSpec(memory_space=pltpu.VMEM)
    operands = list(chunks) + ([square] if keep else [])
    return pl.pallas_call(
        lambda *refs: product_kernel(count, group, keep, *refs),
        out_shape=jax.ShapeDtypeStruct(
            chunks[0].shape, jnp.float32 if keep else jnp.bfloat16
        ),
        in_specs=[pl.BlockSpec(memory_space=pltpu.SMEM)] + [vmem] * (2 + len(operands)),
        out_specs=vmem,
        compiler_params=pltpu.CompilerParams(vmem_limit_bytes=24 * 1024 * 1024),
        cost_estimate=pl.CostEstimate(
            flops=4 * rows * width * lanes * lanes * count,
            bytes_accessed=8 * 1024 * 1024,
            transcendentals=0,
        ),
    )(index, mask, table, *operands)


def gather_parts(parts, axis):
    count = lax.axis_size(axis)
    order = ring_order(count)
    route = [(order[t], order[(t + 1) % count]) for t in range(count)]
    gathered = [[part] for part in parts]
    for _ in range(count - 1):
        for chain in gathered:
            chain.append(lax.ppermute(chain[-1], axis, route))
    return gathered


def gather_table(density, axis):
    rows = lax.axis_size(axis)
    up = [(r, (r + 2) % rows) for r in range(rows)]
    down = [(r, (r - 2) % rows) for r in range(rows)]
    far = [(r, (r + 3) % rows if r % 2 else (r - 3) % rows) for r in range(rows)]
    other = [(r, r ^ 1) for r in range(rows)]
    before = lax.ppermute(density, axis, up)
    after = lax.ppermute(density, axis, down)
    extra = lax.ppermute(density, axis, far)
    near = jnp.concatenate([before, density, after], axis=0)
    return jnp.concatenate([near, lax.ppermute(near, axis, other), extra], axis=0)


def table_slot(distance, row_index, local_rows):
    owner = jnp.floor_divide(distance, local_rows)
    inner = distance - owner * local_rows
    core = jnp.mod(row_index, 2)
    place = owner + core
    pair = jnp.floor_divide(place, 2)
    same = jnp.mod(place, 2) == core
    panel = jnp.where(jnp.abs(pair) == 2, 6, jnp.where(same, pair + 1, pair + 4))
    return panel * local_rows + inner


def shards(density, columns):
    row_index = lax.axis_index("row")
    col_index = lax.axis_index("col")
    local_rows, width, lanes = density.shape
    group = lanes // width
    total, stored = columns.shape
    count = stored // group
    base = row_index * local_rows

    order = ring_order(count)
    arrival = [[0] * count for _ in range(count)]
    for t in range(count):
        arrival[order[t]] = [order[(t - s) % count] for s in range(count)]
    arrival = lax.dynamic_index_in_dim(
        jnp.array(arrival, jnp.int32), col_index, 0, keepdims=False
    )

    own = lax.dynamic_slice_in_dim(columns, base, local_rows, 0)
    goal = lax.dynamic_slice_in_dim(own, col_index * group, group, 1)
    own = jnp.take(own.reshape(local_rows, count, group), arrival, axis=1)
    own = own.reshape(local_rows, stored)
    distance = jnp.mod(own - base + total // 2, total) - total // 2
    index = table_slot(distance, row_index, local_rows).reshape(-1)
    held = lax.dynamic_slice_in_dim(columns, col_index * group, group, 1)
    held = jnp.take(held, own.reshape(-1), axis=0).reshape(local_rows, stored, group)
    lane_slot = jnp.arange(lanes, dtype=jnp.int32) // width
    mine = jnp.where(lane_slot == 0, held[..., :1], held[..., 1:])
    direct = jnp.where(lane_slot == 0, goal[:, None, :1], goal[:, None, 1:])
    swapped = jnp.where(lane_slot == 0, goal[:, None, 1:], goal[:, None, :1])
    mask = jnp.concatenate([mine == direct, mine == swapped], axis=-1)
    mask = mask.astype(jnp.float32).reshape(local_rows * stored, 2 * lanes)

    half = local_rows // PARTS
    cuts = [slice(p * half, (p + 1) * half) for p in range(PARTS)]
    metas = [slice(p * half * stored, (p + 1) * half * stored) for p in range(PARTS)]
    left = gather_parts([density[cut] for cut in cuts], "col")
    table = gather_table(density, "row")
    table = table.reshape(-1, width, lanes)
    squares = [
        product(index[meta], mask[meta], table, chain)
        for meta, chain in zip(metas, left)
    ]
    left = gather_parts(squares, "col")
    outs = [
        product(index[meta], mask[meta], table, chain, square)
        for meta, chain, square in zip(metas, left, squares)
    ]
    return jnp.concatenate(outs, axis=0)


def solution(mesh):
    placed = (P("row", None, "col"), P())
    return jax.shard_map(
        shards, mesh=mesh, in_specs=placed, out_specs=P("row", None, "col"), check_vma=False
    )
```

```python
import jax
import jax.numpy as jnp
import numpy as np
from jax import lax
from jax.experimental import pallas as pl
from jax.experimental.pallas import tpu as pltpu
from jax.sharding import PartitionSpec as P

AXES = ("row", "col")
PANELS = 64
GROUPS = 8
SPAN = 3
TURN = ((0, 3, 1, 2), (1, 2, 0, 3), (2, 0, 3, 1), (3, 1, 2, 0))


def device(half, x, y, core, z):
    return (((half * 4 + x) * 4 + y) * 2 + core) * GROUPS + z


def start(panel, group):
    return panel * GROUPS + group


def between(panel, group):
    half, x, y, core = panel // 32, panel // 8 % 4, panel // 2 % 4, panel % 2
    return device(half, TURN[x][group // 2], panel % 4, y // 2, group)


def place(panel, group):
    half, x = panel // 32, panel // 8 % 4
    return device(half, TURN[x][group // 2], panel % 4, group % 2, panel // 4 % 8)


JOBS = [(panel, group) for panel in range(PANELS) for group in range(GROUPS)]


def route(source, target):
    return sorted((source(*job), target(*job)) for job in JOBS)


def sideways(distance):
    moves = []
    for panel, group in JOBS:
        x = (TURN[panel // 8 % 4][group // 2] - distance) % 4
        other = TURN[panel // 8 % 4].index(x) * 2 + group % 2
        moves.append((place(panel, other), place(panel, group)))
    return sorted(moves)


def arrival(panel, group):
    order = []
    for core in (group % 2, 1 - group % 2):
        for distance in (0, 1, -1, 2):
            x = (TURN[panel // 8 % 4][group // 2] - distance) % 4
            order.append(TURN[panel // 8 % 4].index(x) * 2 + core)
    return order


def send(value, moves):
    return lax.ppermute(value, AXES, moves)


def gather_row(part):
    other = route(place, lambda panel, group: place(panel, group ^ 1))
    near = [part] + [send(part, sideways(distance)) for distance in (1, -1, 2)]
    return near + [send(piece, other) for piece in near]


def gather_table(part):
    panels = []
    for offset in range(-SPAN, SPAN + 1):
        if offset == 0:
            panels.append(part)
        else:
            moves = route(lambda p, g: place((p + offset) % PANELS, g), place)
            panels.append(send(part, moves))
    return jnp.concatenate(panels, axis=0)


def product_kernel(count, group, keep, index_ref, mask_ref, table_ref, *refs):
    chunks = refs[:count]
    out_ref = refs[-1]
    rows, width, lanes = chunks[0].shape
    blocks = count * group
    for i in range(rows):
        total = None
        for step in range(0, count, 2):
            left = jnp.concatenate([chunks[step][i], chunks[step + 1][i]], axis=1)
            pieces = []
            for b in range(step * group, (step + 2) * group):
                piece = table_ref[index_ref[i * blocks + b]]
                piece = jnp.concatenate([piece, piece], axis=1)
                mask = mask_ref[pl.ds(i * blocks + b, 1), :].astype(piece.dtype)
                pieces.append(piece * mask)
            right = jnp.concatenate(pieces, axis=0)
            part = jnp.dot(left, right, preferred_element_type=jnp.float32)
            total = part if total is None else total + part
        value = total[:, :lanes] + pltpu.roll(total[:, lanes:], width, 1)
        if keep:
            value = 3.0 * chunks[0][i].astype(jnp.float32) - 2.0 * value
        out_ref[i] = value.astype(out_ref.dtype)


def product(index, mask, table, chunks, keep):
    count = len(chunks)
    rows, width, lanes = chunks[0].shape
    vmem = pl.BlockSpec(memory_space=pltpu.VMEM)
    return pl.pallas_call(
        lambda *refs: product_kernel(count, lanes // width, keep, *refs),
        out_shape=jax.ShapeDtypeStruct(chunks[0].shape, jnp.bfloat16),
        in_specs=[pl.BlockSpec(memory_space=pltpu.SMEM)] + [vmem] * (2 + count),
        out_specs=vmem,
        compiler_params=pltpu.CompilerParams(vmem_limit_bytes=24 * 1024 * 1024),
        cost_estimate=pl.CostEstimate(
            flops=4 * rows * width * lanes * lanes * count,
            bytes_accessed=8 * 1024 * 1024,
            transcendentals=0,
        ),
    )(index, mask, table, *chunks)


def shards(density, columns):
    local_rows, width, lanes = density.shape
    group = lanes // width
    total, stored = columns.shape

    jobs = np.zeros((PANELS * GROUPS, 2 + GROUPS), np.int32)
    for job in JOBS:
        jobs[place(*job)] = [*job, *arrival(*job)]
    here = lax.axis_index("row") * GROUPS + lax.axis_index("col")
    job = lax.dynamic_index_in_dim(jnp.array(jobs), here, 0, keepdims=False)
    panel, mine, order = job[0], job[1], job[2:]

    part = send(density, route(start, between))
    part = send(part, route(between, place))

    base = panel * local_rows
    own = lax.dynamic_slice_in_dim(columns, base, local_rows, 0)
    goal = lax.dynamic_slice_in_dim(own, mine * group, group, 1)
    own = jnp.take(own.reshape(local_rows, GROUPS, group), order, axis=1)
    own = own.reshape(local_rows, stored)
    distance = jnp.mod(own - base + total // 2, total) - total // 2
    index = (distance + SPAN * local_rows).reshape(-1)
    held = lax.dynamic_slice_in_dim(columns, mine * group, group, 1)
    held = jnp.take(held, own.reshape(-1), axis=0).reshape(local_rows, stored, group)
    lane_slot = jnp.arange(lanes, dtype=jnp.int32) // width
    found = jnp.where(lane_slot == 0, held[..., :1], held[..., 1:])
    direct = jnp.where(lane_slot == 0, goal[:, None, :1], goal[:, None, 1:])
    swapped = jnp.where(lane_slot == 0, goal[:, None, 1:], goal[:, None, :1])
    mask = jnp.concatenate([found == direct, found == swapped], axis=-1)
    mask = mask.astype(jnp.float32).reshape(local_rows * stored, 2 * lanes)

    left = gather_row(part)
    table = gather_table(part).reshape(-1, width, lanes)
    square = product(index, mask, table, left, False)
    result = product(index, mask, table, gather_row(square), True)
    return send(result, route(place, start)).astype(jnp.float32)


def solution(mesh):
    placed = (P("row", None, "col"), P())
    return jax.shard_map(
        shards, mesh=mesh, in_specs=placed, out_specs=P("row", None, "col"), check_vma=False
    )
```

```python
import jax
import jax.numpy as jnp
import numpy as np
from jax import lax
from jax.experimental import pallas as pl
from jax.experimental.pallas import tpu as pltpu
from jax.sharding import PartitionSpec as P

AXES = ("row", "col")
PANELS = 64
GROUPS = 8
TURN = ((0, 3, 1, 2), (1, 2, 0, 3), (2, 0, 3, 1), (3, 1, 2, 0))


def device(half, x, y, core, z):
    return (((half * 4 + x) * 4 + y) * 2 + core) * GROUPS + z


def start(panel, group):
    return panel * GROUPS + group


def between(panel, group):
    half, x, y, core = panel // 32, panel // 8 % 4, panel // 2 % 4, panel % 2
    return device(half, TURN[x][group // 2], panel % 4, y // 2, group)


def place(panel, group):
    half, x = panel // 32, panel // 8 % 4
    return device(half, TURN[x][group // 2], panel % 4, group % 2, panel // 4 % 8)


JOBS = [(panel, group) for panel in range(PANELS) for group in range(GROUPS)]


def route(source, target):
    return sorted((source(*job), target(*job)) for job in JOBS)


def sideways(distance):
    moves = []
    for panel, group in JOBS:
        x = (TURN[panel // 8 % 4][group // 2] - distance) % 4
        other = TURN[panel // 8 % 4].index(x) * 2 + group % 2
        moves.append((place(panel, other), place(panel, group)))
    return sorted(moves)


def arrival(panel, group):
    order = []
    for core in (group % 2, 1 - group % 2):
        for distance in (0, 2, 1, -1):
            x = (TURN[panel // 8 % 4][group // 2] - distance) % 4
            order.append(TURN[panel // 8 % 4].index(x) * 2 + core)
    return order


def send(value, moves):
    return lax.ppermute(value, AXES, moves)


def gather_row(part, after=()):
    other = route(place, lambda panel, group: place(panel, group ^ 1))
    near = [part] + [send(part, sideways(distance)) for distance in (2, 1, -1)]
    near = lax.optimization_barrier((near, after))[0]
    far = send(jnp.concatenate(near, axis=0), other)
    return near + jnp.split(far, len(near), axis=0)


def column_panel(panel, distance):
    return panel // 4 * 4 + (panel + distance) % 4


def passed(panel, distance):
    wanted = column_panel(panel, distance)
    return (wanted - 4 if wanted > panel else wanted + 4) % PANELS


def gather_beside(part):
    beside = []
    for distance in (2, 1, 3):
        moves = route(lambda p, g: place(column_panel(p, distance), g), place)
        beside.append(send(part, moves))
    return beside


def gather_table(part, beside):
    beyond = []
    for distance, piece in zip((2, 1, 3), beside):
        moves = route(
            lambda p, g: place(passed(p, distance) // 4 * 4 + p % 4, g), place
        )
        beyond.append(send(piece, moves))
    return jnp.concatenate([part] + beside + beyond, axis=0)


def table_panel(owner, panel):
    index = jnp.zeros_like(owner)
    for slot, distance in enumerate((2, 1, 3)):
        wanted = column_panel(panel, distance)
        index = jnp.where(owner == wanted - panel, 1 + slot, index)
        outer = jnp.where(wanted > panel, wanted - 4, wanted + 4)
        index = jnp.where(owner == outer - panel, 4 + slot, index)
    return index


def product_kernel(count, group, keep, index_ref, mask_ref, table_ref, *refs):
    chunks = refs[:count]
    out_ref = refs[-1]
    rows, width, lanes = chunks[0].shape
    blocks = count * group
    for i in range(rows):
        total = None
        for step in range(0, count, 2):
            left = jnp.concatenate([chunks[step][i], chunks[step + 1][i]], axis=1)
            pieces = []
            for b in range(step * group, (step + 2) * group):
                piece = table_ref[index_ref[i * blocks + b]]
                piece = jnp.concatenate([piece, piece], axis=1)
                mask = mask_ref[pl.ds(i * blocks + b, 1), :].astype(piece.dtype)
                pieces.append(piece * mask)
            right = jnp.concatenate(pieces, axis=0)
            part = jnp.dot(left, right, preferred_element_type=jnp.float32)
            total = part if total is None else total + part
        value = total[:, :lanes] + pltpu.roll(total[:, lanes:], width, 1)
        if keep:
            value = 3.0 * chunks[0][i].astype(jnp.float32) - 2.0 * value
        out_ref[i] = value.astype(out_ref.dtype)


def product(index, mask, table, chunks, keep):
    count = len(chunks)
    rows, width, lanes = chunks[0].shape
    vmem = pl.BlockSpec(memory_space=pltpu.VMEM)
    return pl.pallas_call(
        lambda *refs: product_kernel(count, lanes // width, keep, *refs),
        out_shape=jax.ShapeDtypeStruct(chunks[0].shape, jnp.bfloat16),
        in_specs=[pl.BlockSpec(memory_space=pltpu.SMEM)] + [vmem] * (2 + count),
        out_specs=vmem,
        compiler_params=pltpu.CompilerParams(vmem_limit_bytes=24 * 1024 * 1024),
        cost_estimate=pl.CostEstimate(
            flops=4 * rows * width * lanes * lanes * count,
            bytes_accessed=8 * 1024 * 1024,
            transcendentals=0,
        ),
    )(index, mask, table, *chunks)


def shards(density, columns):
    local_rows, width, lanes = density.shape
    group = lanes // width
    total, stored = columns.shape

    jobs = np.zeros((PANELS * GROUPS, 2 + GROUPS), np.int32)
    for job in JOBS:
        jobs[place(*job)] = [*job, *arrival(*job)]
    here = lax.axis_index("row") * GROUPS + lax.axis_index("col")
    job = lax.dynamic_index_in_dim(jnp.array(jobs), here, 0, keepdims=False)
    panel, mine, order = job[0], job[1], job[2:]

    part = send(density, route(start, between))
    part = send(part, route(between, place))

    base = panel * local_rows
    own = lax.dynamic_slice_in_dim(columns, base, local_rows, 0)
    goal = lax.dynamic_slice_in_dim(own, mine * group, group, 1)
    own = jnp.take(own.reshape(local_rows, GROUPS, group), order, axis=1)
    own = own.reshape(local_rows, stored)
    distance = jnp.mod(own - base + total // 2, total) - total // 2
    owner = jnp.floor_divide(distance, local_rows)
    index = table_panel(owner, panel) * local_rows + distance - owner * local_rows
    index = index.reshape(-1)
    held = lax.dynamic_slice_in_dim(columns, mine * group, group, 1)
    held = jnp.take(held, own.reshape(-1), axis=0).reshape(local_rows, stored, group)
    lane_slot = jnp.arange(lanes, dtype=jnp.int32) // width
    found = jnp.where(lane_slot == 0, held[..., :1], held[..., 1:])
    direct = jnp.where(lane_slot == 0, goal[:, None, :1], goal[:, None, 1:])
    swapped = jnp.where(lane_slot == 0, goal[:, None, 1:], goal[:, None, :1])
    mask = jnp.concatenate([found == direct, found == swapped], axis=-1)
    mask = mask.astype(jnp.float32).reshape(local_rows * stored, 2 * lanes)

    beside = gather_beside(part)
    left = gather_row(part, beside)
    table = gather_table(part, beside).reshape(-1, width, lanes)
    square = product(index, mask, table, left, False)
    result = product(index, mask, table, gather_row(square), True)
    return send(result, route(place, start)).astype(jnp.float32)


def solution(mesh):
    placed = (P("row", None, "col"), P())
    return jax.shard_map(
        shards, mesh=mesh, in_specs=placed, out_specs=P("row", None, "col"), check_vma=False
    )
```

```python
import jax
import jax.numpy as jnp
import numpy as np
from jax import lax
from jax.experimental import pallas as pl
from jax.experimental.pallas import tpu as pltpu
from jax.sharding import PartitionSpec as P

AXES = ("row", "col")
PANELS = 64
GROUPS = 8
SPOTS = (
    (2, 3, 0, 1), (1, 0, 3, 2), (3, 0, 1, 2), (1, 2, 3, 0),
    (2, 1, 0, 3), (3, 1, 2, 0), (0, 2, 1, 3), (0, 3, 2, 1),
)


def device(half, x, y, core, z):
    return (((half * 4 + x) * 4 + y) * 2 + core) * GROUPS + z


def spot(panel, group):
    return SPOTS[group][panel // 8 % 4]


def held_at(panel, x):
    return [group for group in range(GROUPS) if spot(panel, group) == x % 4]


def lane(panel, group):
    return held_at(panel, spot(panel, group)).index(group)


def start(panel, group):
    return panel * GROUPS + group


def between(panel, group):
    return device(panel // 32, spot(panel, group), panel % 4, panel // 4 % 2, group)


def place(panel, group):
    x = spot(panel, group)
    return device(panel // 32, x, panel % 4, lane(panel, group), panel // 4 % 8)


JOBS = [(panel, group) for panel in range(PANELS) for group in range(GROUPS)]


def route(source, target):
    return sorted((source(*job), target(*job)) for job in JOBS)


def beside(panel, group, distance):
    return held_at(panel, spot(panel, group) - distance)[lane(panel, group)]


def opposite(panel, group):
    return held_at(panel, spot(panel, group))[1 - lane(panel, group)]


def arrival(panel, group):
    near = [beside(panel, group, distance) for distance in (0, 2, 1, -1)]
    return near + [opposite(panel, other) for other in near]


def column_panel(panel, distance):
    return panel // 4 * 4 + (panel + distance) % 4


def send(value, source):
    return lax.ppermute(value, AXES, route(source, place))


def gather_row(part, after=()):
    near = [part]
    for distance in (2, 1, -1):
        near.append(send(part, lambda p, g: place(p, beside(p, g, distance))))
    near = lax.optimization_barrier((near, after))[0]
    far = send(jnp.concatenate(near, axis=0), lambda p, g: place(p, opposite(p, g)))
    return near + jnp.split(far, len(near), axis=0)


def gather_column(part):
    return [
        send(part, lambda p, g: place(column_panel(p, distance), g))
        for distance in (2, 1, 3)
    ]


def gather_table(part, column, panel):
    low = panel % 4 < 2
    two, one, three = column
    pair = jnp.concatenate([two, jnp.where(low, one, three)], axis=0)
    rest = jnp.where(low, three, one)
    pair = send(pair, lambda p, g: place((p + (-4 if p % 4 < 2 else 4)) % PANELS, g))
    rest = send(rest, lambda p, g: place((p + (4 if p % 2 else -4)) % PANELS, g))
    return jnp.concatenate([part, two, one, three, pair, rest], axis=0)


def table_panel(owner, panel):
    y = panel % 4
    index = jnp.zeros_like(owner)
    for slot, distance in enumerate((2, 1, 3)):
        same = (y + distance) % 4 - y
        index = jnp.where(owner == same, 1 + slot, index)
        outer = jnp.where(same > 0, same - 4, same + 4)
        swap = jnp.where(y < 2, 4 + slot, 7 - slot) if slot else 4
        index = jnp.where(owner == outer, swap, index)
    return index


def product_kernel(count, group, keep, index_ref, mask_ref, table_ref, *refs):
    chunks = refs[:count]
    out_ref = refs[-1]
    rows, width, lanes = chunks[0].shape
    blocks = count * group
    for i in range(rows):
        total = None
        for step in range(0, count, 2):
            left = jnp.concatenate([chunks[step][i], chunks[step + 1][i]], axis=1)
            pieces = []
            for b in range(step * group, (step + 2) * group):
                piece = table_ref[index_ref[i * blocks + b]]
                piece = jnp.concatenate([piece, piece], axis=1)
                mask = mask_ref[pl.ds(i * blocks + b, 1), :].astype(piece.dtype)
                pieces.append(piece * mask)
            right = jnp.concatenate(pieces, axis=0)
            part = jnp.dot(left, right, preferred_element_type=jnp.float32)
            total = part if total is None else total + part
        value = total[:, :lanes] + pltpu.roll(total[:, lanes:], width, 1)
        if keep:
            value = 3.0 * chunks[0][i].astype(jnp.float32) - 2.0 * value
        out_ref[i] = value.astype(out_ref.dtype)


def product(index, mask, table, chunks, keep):
    count = len(chunks)
    rows, width, lanes = chunks[0].shape
    vmem = pl.BlockSpec(memory_space=pltpu.VMEM)
    return pl.pallas_call(
        lambda *refs: product_kernel(count, lanes // width, keep, *refs),
        out_shape=jax.ShapeDtypeStruct(chunks[0].shape, jnp.bfloat16),
        in_specs=[pl.BlockSpec(memory_space=pltpu.SMEM)] + [vmem] * (2 + count),
        out_specs=vmem,
        compiler_params=pltpu.CompilerParams(vmem_limit_bytes=24 * 1024 * 1024),
        cost_estimate=pl.CostEstimate(
            flops=4 * rows * width * lanes * lanes * count,
            bytes_accessed=8 * 1024 * 1024,
            transcendentals=0,
        ),
    )(index, mask, table, *chunks)


def shards(density, columns):
    local_rows, width, lanes = density.shape
    group = lanes // width
    total, stored = columns.shape

    jobs = np.zeros((PANELS * GROUPS, 2 + GROUPS), np.int32)
    for job in JOBS:
        jobs[place(*job)] = [*job, *arrival(*job)]
    here = lax.axis_index("row") * GROUPS + lax.axis_index("col")
    job = lax.dynamic_index_in_dim(jnp.array(jobs), here, 0, keepdims=False)
    panel, mine, order = job[0], job[1], job[2:]

    part = lax.ppermute(density, AXES, route(start, between))

    base = panel * local_rows
    own = lax.dynamic_slice_in_dim(columns, base, local_rows, 0)
    goal = lax.dynamic_slice_in_dim(own, mine * group, group, 1)
    own = jnp.take(own.reshape(local_rows, GROUPS, group), order, axis=1)
    own = own.reshape(local_rows, stored)
    distance = jnp.mod(own - base + total // 2, total) - total // 2
    owner = jnp.floor_divide(distance, local_rows)
    index = table_panel(owner, panel) * local_rows + distance - owner * local_rows
    index = index.reshape(-1)
    held = lax.dynamic_slice_in_dim(columns, mine * group, group, 1)
    held = jnp.take(held, own.reshape(-1), axis=0).reshape(local_rows, stored, group)
    lane_slot = jnp.arange(lanes, dtype=jnp.int32) // width
    found = jnp.where(lane_slot == 0, held[..., :1], held[..., 1:])
    direct = jnp.where(lane_slot == 0, goal[:, None, :1], goal[:, None, 1:])
    swapped = jnp.where(lane_slot == 0, goal[:, None, 1:], goal[:, None, :1])
    mask = jnp.concatenate([found == direct, found == swapped], axis=-1)
    mask = mask.astype(jnp.float32).reshape(local_rows * stored, 2 * lanes)

    part, index, mask = lax.optimization_barrier((part, index, mask))
    part = send(part, between)

    column = gather_column(part)
    left = gather_row(part, column)
    table = gather_table(part, column, panel).reshape(-1, width, lanes)
    square = product(index, mask, table, left, False)
    result = product(index, mask, table, gather_row(square), True)
    return lax.ppermute(result, AXES, route(place, start)).astype(jnp.float32)


def solution(mesh):
    placed = (P("row", None, "col"), P())
    return jax.shard_map(
        shards, mesh=mesh, in_specs=placed, out_specs=P("row", None, "col"), check_vma=False
    )
```

```python
import jax
import jax.numpy as jnp
import numpy as np
from jax import lax
from jax.experimental import pallas as pl
from jax.experimental.pallas import tpu as pltpu
from jax.sharding import PartitionSpec as P

AXES = ("row", "col")
PANELS = 64
GROUPS = 8
SPOTS = (
    (2, 3, 0, 1), (1, 0, 3, 2), (3, 0, 1, 2), (1, 2, 3, 0),
    (2, 1, 0, 3), (3, 1, 2, 0), (0, 2, 1, 3), (0, 3, 2, 1),
)


def device(half, x, y, core, z):
    return (((half * 4 + x) * 4 + y) * 2 + core) * GROUPS + z


def spot(panel, group):
    return SPOTS[group][panel // 8 % 4]


def held_at(panel, x):
    return [group for group in range(GROUPS) if spot(panel, group) == x % 4]


def lane(panel, group):
    return held_at(panel, spot(panel, group)).index(group)


def start(panel, group):
    return panel * GROUPS + group


def between(panel, group):
    return device(panel // 32, spot(panel, group), panel % 4, panel // 4 % 2, group)


def place(panel, group):
    x = spot(panel, group)
    return device(panel // 32, x, panel % 4, lane(panel, group), panel // 4 % 8)


JOBS = [(panel, group) for panel in range(PANELS) for group in range(GROUPS)]


def route(source, target):
    return sorted((source(*job), target(*job)) for job in JOBS)


def beside(panel, group, distance):
    return held_at(panel, spot(panel, group) - distance)[lane(panel, group)]


def opposite(panel, group):
    return held_at(panel, spot(panel, group))[1 - lane(panel, group)]


def plane_order(panel, group):
    return [group for x in range(4) for group in held_at(panel, x)]


def arrival(panel, group):
    near = [beside(panel, group, distance) for distance in (0, 2, 1, -1)]
    return near + [opposite(panel, other) for other in near]


def column_panel(panel, distance):
    return panel // 4 * 4 + (panel + distance) % 4


def send(value, source):
    return lax.ppermute(value, AXES, route(source, place))


def gather_plane(part):
    planes = [
        [device(half, x, y, core, 0) // GROUPS for x in range(4) for core in range(2)]
        for half in range(2)
        for y in range(4)
    ]
    return lax.all_gather(part, "row", axis=0, tiled=True, axis_index_groups=planes)


def gather_row(part):
    near = [part]
    for distance in (2, 1, -1):
        near.append(send(part, lambda p, g: place(p, beside(p, g, distance))))
    far = send(jnp.concatenate(near, axis=0), lambda p, g: place(p, opposite(p, g)))
    return near + jnp.split(far, len(near), axis=0)


def gather_column(part):
    return [
        send(part, lambda p, g: place(column_panel(p, distance), g))
        for distance in (2, 1, 3)
    ]


def gather_table(part, column, panel):
    low = panel % 4 < 2
    two, one, three = column
    pair = jnp.concatenate([two, jnp.where(low, one, three)], axis=0)
    rest = jnp.where(low, three, one)
    pair = send(pair, lambda p, g: place((p + (-4 if p % 4 < 2 else 4)) % PANELS, g))
    rest = send(rest, lambda p, g: place((p + (4 if p % 2 else -4)) % PANELS, g))
    return jnp.concatenate([part, two, one, three, pair, rest], axis=0)


def table_panel(owner, panel):
    y = panel % 4
    index = jnp.zeros_like(owner)
    for slot, distance in enumerate((2, 1, 3)):
        same = (y + distance) % 4 - y
        index = jnp.where(owner == same, 1 + slot, index)
        outer = jnp.where(same > 0, same - 4, same + 4)
        swap = jnp.where(y < 2, 4 + slot, 7 - slot) if slot else 4
        index = jnp.where(owner == outer, swap, index)
    return index


def product_kernel(count, group, keep, index_ref, mask_ref, table_ref, *refs):
    out_ref = refs[-1]
    rows, width, lanes = out_ref.shape
    chunks = [ref.at[pl.ds(j, rows)] for ref in refs[:-1] for j in range(0, ref.shape[0], rows)]
    blocks = count * group
    for i in range(rows):
        total = None
        for step in range(0, count, 2):
            left = jnp.concatenate([chunks[step][i], chunks[step + 1][i]], axis=1)
            pieces = []
            for b in range(step * group, (step + 2) * group):
                piece = table_ref[index_ref[i * blocks + b]]
                piece = jnp.concatenate([piece, piece], axis=1)
                mask = mask_ref[pl.ds(i * blocks + b, 1), :].astype(piece.dtype)
                pieces.append(piece * mask)
            right = jnp.concatenate(pieces, axis=0)
            part = jnp.dot(left, right, preferred_element_type=jnp.float32)
            total = part if total is None else total + part
        value = total[:, :lanes] + pltpu.roll(total[:, lanes:], width, 1)
        if keep:
            value = 3.0 * chunks[0][i].astype(jnp.float32) - 2.0 * value
        out_ref[i] = value.astype(out_ref.dtype)


def product(index, mask, table, chunks, rows, keep):
    width, lanes = table.shape[1:]
    count = sum(chunk.shape[0] for chunk in chunks) // rows
    vmem = pl.BlockSpec(memory_space=pltpu.VMEM)
    return pl.pallas_call(
        lambda *refs: product_kernel(count, lanes // width, keep, *refs),
        out_shape=jax.ShapeDtypeStruct((rows, width, lanes), jnp.bfloat16),
        in_specs=[pl.BlockSpec(memory_space=pltpu.SMEM)] + [vmem] * (2 + len(chunks)),
        out_specs=vmem,
        compiler_params=pltpu.CompilerParams(vmem_limit_bytes=24 * 1024 * 1024),
        cost_estimate=pl.CostEstimate(
            flops=4 * rows * width * lanes * lanes * count,
            bytes_accessed=8 * 1024 * 1024,
            transcendentals=0,
        ),
    )(index, mask, table, *chunks)


def shards(density, columns):
    local_rows, width, lanes = density.shape
    group = lanes // width
    total, stored = columns.shape

    jobs = np.zeros((PANELS * GROUPS, 2 + 2 * GROUPS), np.int32)
    for job in JOBS:
        jobs[place(*job)] = [*job, *plane_order(*job), *arrival(*job)]
    here = lax.axis_index("row") * GROUPS + lax.axis_index("col")
    job = lax.dynamic_index_in_dim(jnp.array(jobs), here, 0, keepdims=False)
    panel, mine = job[0], job[1]

    part = lax.ppermute(density, AXES, route(start, between))

    base = panel * local_rows
    own = lax.dynamic_slice_in_dim(columns, base, local_rows, 0)
    goal = lax.dynamic_slice_in_dim(own, mine * group, group, 1)
    orders = job[2:].reshape(2, GROUPS)
    own = jnp.take(own.reshape(local_rows, GROUPS, group), orders, axis=1)
    own = own.swapaxes(0, 1).reshape(2, local_rows, stored)
    distance = jnp.mod(own - base + total // 2, total) - total // 2
    owner = jnp.floor_divide(distance, local_rows)
    index = table_panel(owner, panel) * local_rows + distance - owner * local_rows
    index = index.reshape(2, -1)
    held = lax.dynamic_slice_in_dim(columns, mine * group, group, 1)
    held = jnp.take(held, own.reshape(-1), axis=0).reshape(2, local_rows, stored, group)
    lane_slot = jnp.arange(lanes, dtype=jnp.int32) // width
    found = jnp.where(lane_slot == 0, held[..., :1], held[..., 1:])
    direct = jnp.where(lane_slot == 0, goal[:, None, :1], goal[:, None, 1:])
    swapped = jnp.where(lane_slot == 0, goal[:, None, 1:], goal[:, None, :1])
    mask = jnp.concatenate([found == direct, found == swapped], axis=-1)
    mask = mask.astype(jnp.float32).reshape(2, local_rows * stored, 2 * lanes)
    part, index, mask = lax.optimization_barrier((part, index, mask))
    part = send(part, between)

    left = gather_plane(part)
    table = gather_table(part, gather_column(part), panel).reshape(-1, width, lanes)
    square = product(index[0], mask[0], table, [left], local_rows, False)
    left = gather_row(square)
    result = product(index[1], mask[1], table, left, local_rows, True)
    return lax.ppermute(result, AXES, route(place, start)).astype(jnp.float32)


def solution(mesh):
    placed = (P("row", None, "col"), P())
    return jax.shard_map(
        shards, mesh=mesh, in_specs=placed, out_specs=P("row", None, "col"), check_vma=False
    )
```

```python
import jax
import jax.numpy as jnp
import numpy as np
from jax import lax
from jax.experimental import pallas as pl
from jax.experimental.pallas import tpu as pltpu
from jax.sharding import PartitionSpec as P

AXES = ("row", "col")
PANELS = 64
GROUPS = 8
SPOTS = (
    (2, 3, 0, 1), (1, 0, 3, 2), (3, 0, 1, 2), (1, 2, 3, 0),
    (2, 1, 0, 3), (3, 1, 2, 0), (0, 2, 1, 3), (0, 3, 2, 1),
)


def device(half, x, y, core, z):
    return (((half * 4 + x) * 4 + y) * 2 + core) * GROUPS + z


def spot(panel, group):
    return SPOTS[group][panel // 8 % 4]


def held_at(panel, x):
    return [group for group in range(GROUPS) if spot(panel, group) == x % 4]


def lane(panel, group):
    return held_at(panel, spot(panel, group)).index(group)


def start(panel, group):
    return panel * GROUPS + group


def between(panel, group):
    return device(panel // 32, spot(panel, group), panel % 4, panel // 4 % 2, group)


def place(panel, group):
    x = spot(panel, group)
    return device(panel // 32, x, panel % 4, lane(panel, group), panel // 4 % 8)


JOBS = [(panel, group) for panel in range(PANELS) for group in range(GROUPS)]


def route(source, target):
    return sorted((source(*job), target(*job)) for job in JOBS)


def beside(panel, group, distance):
    return held_at(panel, spot(panel, group) - distance)[lane(panel, group)]


def opposite(panel, group):
    return held_at(panel, spot(panel, group))[1 - lane(panel, group)]


def arrival(panel, group):
    near = [beside(panel, group, distance) for distance in (0, 2, 1, -1)]
    return near + [opposite(panel, other) for other in near]


def column_panel(panel, distance):
    return panel // 4 * 4 + (panel + distance) % 4


def send(value, source):
    return lax.ppermute(value, AXES, route(source, place))


def gather_row(near):
    far = send(jnp.concatenate(near, axis=0), lambda p, g: place(p, opposite(p, g)))
    return near + jnp.split(far, len(near), axis=0)


def gather_beside(part, distances):
    return [
        send(part, lambda p, g: place(p, beside(p, g, distance)))
        for distance in distances
    ]


def gather_column(part):
    return [
        send(part, lambda p, g: place(column_panel(p, distance), g))
        for distance in (2, 1, 3)
    ]


def rows_to_pass(column, panel):
    low = panel % 4 < 2
    two, one, three = column
    pair = jnp.concatenate([two, jnp.where(low, one, three)], axis=0)
    return pair, jnp.where(low, three, one)


def pass_rows(pair, rest):
    pair = send(pair, lambda p, g: place((p + (-4 if p % 4 < 2 else 4)) % PANELS, g))
    rest = send(rest, lambda p, g: place((p + (4 if p % 2 else -4)) % PANELS, g))
    return [pair, rest]


def table_panel(owner, panel):
    y = panel % 4
    index = jnp.zeros_like(owner)
    for slot, distance in enumerate((2, 1, 3)):
        same = (y + distance) % 4 - y
        index = jnp.where(owner == same, 1 + slot, index)
        outer = jnp.where(same > 0, same - 4, same + 4)
        swap = jnp.where(y < 2, 4 + slot, 7 - slot) if slot else 4
        index = jnp.where(owner == outer, swap, index)
    return index


def product_kernel(count, group, keep, index_ref, mask_ref, table_ref, *refs):
    chunks = refs[:count]
    out_ref = refs[-1]
    rows, width, lanes = chunks[0].shape
    blocks = count * group
    for i in range(rows):
        total = None
        for step in range(0, count, 2):
            left = jnp.concatenate([chunks[step][i], chunks[step + 1][i]], axis=1)
            pieces = []
            for b in range(step * group, (step + 2) * group):
                piece = table_ref[index_ref[i * blocks + b]]
                piece = jnp.concatenate([piece, piece], axis=1)
                mask = mask_ref[pl.ds(i * blocks + b, 1), :].astype(piece.dtype)
                pieces.append(piece * mask)
            right = jnp.concatenate(pieces, axis=0)
            part = jnp.dot(left, right, preferred_element_type=jnp.float32)
            total = part if total is None else total + part
        value = total[:, :lanes] + pltpu.roll(total[:, lanes:], width, 1)
        if keep:
            value = 3.0 * chunks[0][i].astype(jnp.float32) - 2.0 * value
        out_ref[i] = value.astype(out_ref.dtype)


def product(index, mask, table, chunks, keep):
    count = len(chunks)
    rows, width, lanes = chunks[0].shape
    vmem = pl.BlockSpec(memory_space=pltpu.VMEM)
    return pl.pallas_call(
        lambda *refs: product_kernel(count, lanes // width, keep, *refs),
        out_shape=jax.ShapeDtypeStruct(chunks[0].shape, jnp.bfloat16),
        in_specs=[pl.BlockSpec(memory_space=pltpu.SMEM)] + [vmem] * (2 + count),
        out_specs=vmem,
        compiler_params=pltpu.CompilerParams(vmem_limit_bytes=24 * 1024 * 1024),
        cost_estimate=pl.CostEstimate(
            flops=4 * rows * width * lanes * lanes * count,
            bytes_accessed=8 * 1024 * 1024,
            transcendentals=0,
        ),
    )(index, mask, table, *chunks)


def shards(density, columns):
    local_rows, width, lanes = density.shape
    group = lanes // width
    total, stored = columns.shape

    jobs = np.zeros((PANELS * GROUPS, 2 + GROUPS), np.int32)
    for job in JOBS:
        jobs[place(*job)] = [*job, *arrival(*job)]
    here = lax.axis_index("row") * GROUPS + lax.axis_index("col")
    job = lax.dynamic_index_in_dim(jnp.array(jobs), here, 0, keepdims=False)
    panel, mine, order = job[0], job[1], job[2:]

    part = lax.ppermute(density, AXES, route(start, between))
    part, columns = lax.optimization_barrier((part, columns))
    part = send(part, between)

    base = panel * local_rows
    own = lax.dynamic_slice_in_dim(columns, base, local_rows, 0)
    goal = lax.dynamic_slice_in_dim(own, mine * group, group, 1)
    own = jnp.take(own.reshape(local_rows, GROUPS, group), order, axis=1)
    own = own.reshape(local_rows, stored)
    distance = jnp.mod(own - base + total // 2, total) - total // 2
    owner = jnp.floor_divide(distance, local_rows)
    index = table_panel(owner, panel) * local_rows + distance - owner * local_rows
    index = index.reshape(-1)
    held = lax.dynamic_slice_in_dim(columns, mine * group, group, 1)
    held = jnp.take(held, own.reshape(-1), axis=0).reshape(local_rows, stored, group)
    lane_slot = jnp.arange(lanes, dtype=jnp.int32) // width
    found = jnp.where(lane_slot == 0, held[..., :1], held[..., 1:])
    direct = jnp.where(lane_slot == 0, goal[:, None, :1], goal[:, None, 1:])
    swapped = jnp.where(lane_slot == 0, goal[:, None, 1:], goal[:, None, :1])
    mask = jnp.concatenate([found == direct, found == swapped], axis=-1)
    mask = mask.astype(jnp.float32).reshape(local_rows * stored, 2 * lanes)

    part, index, mask = lax.optimization_barrier((part, index, mask))

    column = gather_column(part)
    near = [part] + gather_beside(part, (2,))
    pair, rest = rows_to_pass(column, panel)
    part, pair, rest = lax.optimization_barrier((part, pair, rest))
    outer = pass_rows(pair, rest)
    near = near + gather_beside(part, (1, -1))
    near, outer = lax.optimization_barrier((near, outer))
    left = gather_row(near)
    table = jnp.concatenate(near[:1] + column + outer, axis=0)
    table = table.reshape(-1, width, lanes)
    square = product(index, mask, table, left, False)
    left = gather_row([square] + gather_beside(square, (2, 1, -1)))
    result = product(index, mask, table, left, True)
    return lax.ppermute(result, AXES, route(place, start)).astype(jnp.float32)


def solution(mesh):
    placed = (P("row", None, "col"), P())
    return jax.shard_map(
        shards, mesh=mesh, in_specs=placed, out_specs=P("row", None, "col"), check_vma=False
    )
```

```python
import jax
import jax.numpy as jnp
import numpy as np
from jax import lax
from jax.experimental import pallas as pl
from jax.experimental.pallas import tpu as pltpu
from jax.sharding import PartitionSpec as P

AXES = ("row", "col")
PIECES = 5
PANELS = 64
GROUPS = 8
SPOTS = (
    (2, 3, 0, 1), (1, 0, 3, 2), (3, 0, 1, 2), (1, 2, 3, 0),
    (2, 1, 0, 3), (3, 1, 2, 0), (0, 2, 1, 3), (0, 3, 2, 1),
)


def device(half, x, y, core, z):
    return (((half * 4 + x) * 4 + y) * 2 + core) * GROUPS + z


def spot(panel, group):
    return SPOTS[group][panel // 8 % 4]


def held_at(panel, x):
    return [group for group in range(GROUPS) if spot(panel, group) == x % 4]


def lane(panel, group):
    return held_at(panel, spot(panel, group)).index(group)


def start(panel, group):
    return panel * GROUPS + group


def between(panel, group):
    return device(panel // 32, spot(panel, group), panel % 4, panel // 4 % 2, group)


def place(panel, group):
    x = spot(panel, group)
    return device(panel // 32, x, panel % 4, lane(panel, group), panel // 4 % 8)


JOBS = [(panel, group) for panel in range(PANELS) for group in range(GROUPS)]


def route(source, target):
    return sorted((source(*job), target(*job)) for job in JOBS)


def opposite(panel, group):
    return held_at(panel, spot(panel, group))[1 - lane(panel, group)]


def arrival(panel, group):
    mine = lane(panel, group)
    return [held_at(panel, x)[core] for core in (mine, 1 - mine) for x in range(4)]


def send(value, source):
    return lax.ppermute(value, AXES, route(source, place))


def gather_ring(part, ring):
    copies = jnp.concatenate([part] * 4, axis=0)
    return lax.all_to_all(copies, "row", 0, 0, tiled=True, axis_index_groups=ring)


X_RINGS = [
    [device(half, x, y, core, 0) // GROUPS for x in range(4)]
    for half in range(2) for y in range(4) for core in range(2)
]
def gather_row(near):
    return [near, send(near, lambda p, g: place(p, opposite(p, g)))]


def gather_column(part):
    return [
        send(part, lambda p, g: place(p // 4 * 4 + (p % 4 ^ flip), g))
        for flip in (1, 2, 3)
    ]


def pass_rows(pair, rest):
    pair = send(pair, lambda p, g: place((p + (-4 if p % 4 < 2 else 4)) % PANELS, g))
    rest = send(rest, lambda p, g: place((p + (4 if p % 2 else -4)) % PANELS, g))
    return pair, rest


def table_panel(owner, panel):
    y = panel % 4
    place_y = y + owner
    inner = jnp.mod(place_y, 4)
    flip = jnp.bitwise_xor(inner, y)
    return jnp.where(place_y == inner, flip, jnp.where(flip == 1, 6, flip + 2))


def product_kernel(count, group, keep, index_ref, mask_ref, *refs):
    out_ref, table_ref = refs[-2:]
    rows, width, lanes = out_ref.shape
    filled = 0
    for ref in refs[:PIECES]:
        table_ref[pl.ds(filled, ref.shape[0])] = ref[...]
        filled += ref.shape[0]
    refs = refs[PIECES:]
    chunks = [
        ref.at[pl.ds(j * rows, rows)]
        for ref in refs[:2]
        for j in range(ref.shape[0] // rows)
    ]
    blocks = count * group
    for i in range(rows):
        total = None
        for step in range(0, count, 2):
            left = jnp.concatenate([chunks[step][i], chunks[step + 1][i]], axis=1)
            pieces = []
            for b in range(step * group, (step + 2) * group):
                piece = table_ref[index_ref[i * blocks + b]]
                piece = jnp.concatenate([piece, piece], axis=1)
                mask = mask_ref[pl.ds(i * blocks + b, 1), :].astype(piece.dtype)
                pieces.append(piece * mask)
            right = jnp.concatenate(pieces, axis=0)
            part = jnp.dot(left, right, preferred_element_type=jnp.float32)
            total = part if total is None else total + part
        value = total[:, :lanes] + pltpu.roll(total[:, lanes:], width, 1)
        if keep:
            value = 3.0 * refs[2][i].astype(jnp.float32) - 2.0 * value
        out_ref[i] = value.astype(out_ref.dtype)


def product(index, mask, table, chunks, rows, keep):
    width, lanes = chunks[0].shape[1:]
    count = sum(chunk.shape[0] for chunk in chunks[:2]) // rows
    vmem = pl.BlockSpec(memory_space=pltpu.VMEM)
    return pl.pallas_call(
        lambda *refs: product_kernel(count, lanes // width, keep, *refs),
        out_shape=jax.ShapeDtypeStruct((rows, width, lanes), jnp.bfloat16),
        in_specs=[pl.BlockSpec(memory_space=pltpu.SMEM)]
        + [vmem] * (1 + len(table) + len(chunks)),
        out_specs=vmem,
        scratch_shapes=[
            pltpu.VMEM((sum(piece.shape[0] for piece in table), width, lanes), jnp.bfloat16)
        ],
        compiler_params=pltpu.CompilerParams(vmem_limit_bytes=24 * 1024 * 1024),
        cost_estimate=pl.CostEstimate(
            flops=4 * rows * width * lanes * lanes * count,
            bytes_accessed=8 * 1024 * 1024,
            transcendentals=0,
        ),
    )(index, mask, *table, *chunks)


def shards(density, columns):
    local_rows, width, lanes = density.shape
    group = lanes // width
    total, stored = columns.shape

    jobs = np.zeros((PANELS * GROUPS, 2 + GROUPS), np.int32)
    for job in JOBS:
        jobs[place(*job)] = [*job, *arrival(*job)]
    here = lax.axis_index("row") * GROUPS + lax.axis_index("col")
    job = lax.dynamic_index_in_dim(jnp.array(jobs), here, 0, keepdims=False)
    panel, mine, order = job[0], job[1], job[2:]

    base = panel * local_rows
    own = lax.dynamic_slice_in_dim(columns, base, local_rows, 0)
    goal = lax.dynamic_slice_in_dim(own, mine * group, group, 1)
    held = lax.dynamic_slice_in_dim(columns, mine * group, group, 1)
    own = jnp.take(own.reshape(local_rows, GROUPS, group), order, axis=1)
    own = own.reshape(local_rows, stored)
    distance = jnp.mod(own - base + total // 2, total) - total // 2
    owner = jnp.floor_divide(distance, local_rows)
    index = table_panel(owner, panel) * local_rows + distance - owner * local_rows
    index = index.reshape(-1)

    part = lax.ppermute(density, AXES, route(start, between))
    part, own, goal, held, index = lax.optimization_barrier((part, own, goal, held, index))
    part = send(part, between)

    held = jnp.take(held, own.reshape(-1), axis=0).reshape(local_rows, stored, group)
    lane_slot = jnp.arange(lanes, dtype=jnp.int32) // width
    found = jnp.where(lane_slot == 0, held[..., :1], held[..., 1:])
    direct = jnp.where(lane_slot == 0, goal[:, None, :1], goal[:, None, 1:])
    swapped = jnp.where(lane_slot == 0, goal[:, None, 1:], goal[:, None, :1])
    mask = jnp.concatenate([found == direct, found == swapped], axis=-1)
    mask = mask.astype(jnp.float32).reshape(local_rows * stored, 2 * lanes)

    part, index, mask = lax.optimization_barrier((part, index, mask))

    one, two, three = gather_column(part)
    pair = jnp.concatenate([two, three], axis=0)
    outer, rest = pass_rows(pair, one)
    near = gather_ring(part, X_RINGS)
    near, outer, rest = lax.optimization_barrier((near, outer, rest))
    left = gather_row(near)
    table = [part, one, pair, outer, rest]
    square = product(index, mask, table, left, local_rows, False)
    left = gather_row(gather_ring(square, X_RINGS))
    result = product(index, mask, table, left + [square], local_rows, True)
    return lax.ppermute(result, AXES, route(place, start)).astype(jnp.float32)


def solution(mesh):
    placed = (P("row", None, "col"), P())
    return jax.shard_map(
        shards, mesh=mesh, in_specs=placed, out_specs=P("row", None, "col"), check_vma=False
    )
```

```python
import jax
import jax.numpy as jnp
import numpy as np
from jax import lax
from jax.experimental import pallas as pl
from jax.experimental.pallas import tpu as pltpu
from jax.sharding import PartitionSpec as P

AXES = ("row", "col")
PIECES = 5
PANELS = 64
GROUPS = 8
SPOTS = (
    (2, 3, 0, 1), (1, 0, 3, 2), (3, 0, 1, 2), (1, 2, 3, 0),
    (2, 1, 0, 3), (3, 1, 2, 0), (0, 2, 1, 3), (0, 3, 2, 1),
)


def device(half, x, y, core, z):
    return (((half * 4 + x) * 4 + y) * 2 + core) * GROUPS + z


def spot(panel, group):
    return SPOTS[group][panel // 8 % 4]


def held_at(panel, x):
    return [group for group in range(GROUPS) if spot(panel, group) == x % 4]


def lane(panel, group):
    return held_at(panel, spot(panel, group)).index(group)


def start(panel, group):
    return panel * GROUPS + group


def between(panel, group):
    return device(panel // 32, spot(panel, group), panel % 4, panel // 4 % 2, group)


def place(panel, group):
    x = spot(panel, group)
    return device(panel // 32, x, panel % 4, lane(panel, group), panel // 4 % 8)


JOBS = [(panel, group) for panel in range(PANELS) for group in range(GROUPS)]


def route(source, target):
    return sorted((source(*job), target(*job)) for job in JOBS)


def opposite(panel, group):
    return held_at(panel, spot(panel, group))[1 - lane(panel, group)]


def arrival(panel, group):
    mine = lane(panel, group)
    return [held_at(panel, x)[core] for core in (mine, 1 - mine) for x in range(4)]


def send(value, source):
    return lax.ppermute(value, AXES, route(source, place))


def gather_ring(part, ring):
    copies = jnp.concatenate([part] * 4, axis=0)
    return lax.all_to_all(copies, "row", 0, 0, tiled=True, axis_index_groups=ring)


X_RINGS = [
    [device(half, x, y, core, 0) // GROUPS for x in range(4)]
    for half in range(2) for y in range(4) for core in range(2)
]
def gather_row(near):
    return [near, send(near, lambda p, g: place(p, opposite(p, g)))]


def gather_column(part):
    return [
        send(part, lambda p, g: place(p // 4 * 4 + (p % 4 ^ flip), g))
        for flip in (1, 2, 3)
    ]


def pass_rows(pair, rest):
    pair = send(pair, lambda p, g: place((p + (-4 if p % 4 < 2 else 4)) % PANELS, g))
    rest = send(rest, lambda p, g: place((p + (4 if p % 2 else -4)) % PANELS, g))
    return pair, rest


def table_panel(owner, panel):
    y = panel % 4
    place_y = y + owner
    inner = jnp.mod(place_y, 4)
    flip = jnp.bitwise_xor(inner, y)
    return jnp.where(place_y == inner, flip, jnp.where(flip == 1, 6, flip + 2))


def product_kernel(count, group, keep, index_ref, mask_ref, *refs):
    out_ref, table_ref = refs[-2:]
    rows, width, lanes = out_ref.shape
    filled = 0
    for ref in refs[:PIECES]:
        table_ref[pl.ds(filled, ref.shape[0])] = ref[...]
        filled += ref.shape[0]
    refs = refs[PIECES:]
    chunks = [
        ref.at[pl.ds(j * rows, rows)]
        for ref in refs[:2]
        for j in range(ref.shape[0] // rows)
    ]
    blocks = count * group
    for i in range(rows):
        total = None
        for step in range(0, count, 2):
            left = jnp.concatenate([chunks[step][i], chunks[step + 1][i]], axis=1)
            pieces = []
            for b in range(step * group, (step + 2) * group):
                piece = table_ref[index_ref[i * blocks + b]]
                piece = jnp.concatenate([piece, piece], axis=1)
                mask = mask_ref[pl.ds(i * blocks + b, 1), :].astype(piece.dtype)
                pieces.append(piece * mask)
            right = jnp.concatenate(pieces, axis=0)
            part = jnp.dot(left, right, preferred_element_type=jnp.float32)
            total = part if total is None else total + part
        value = total[:, :lanes] + pltpu.roll(total[:, lanes:], width, 1)
        if keep:
            value = 3.0 * refs[2][i].astype(jnp.float32) - 2.0 * value
        out_ref[i] = value.astype(out_ref.dtype)


def product(index, mask, table, chunks, rows, keep):
    width, lanes = chunks[0].shape[1:]
    count = sum(chunk.shape[0] for chunk in chunks[:2]) // rows
    vmem = pl.BlockSpec(memory_space=pltpu.VMEM)
    return pl.pallas_call(
        lambda *refs: product_kernel(count, lanes // width, keep, *refs),
        out_shape=jax.ShapeDtypeStruct((rows, width, lanes), jnp.bfloat16),
        in_specs=[pl.BlockSpec(memory_space=pltpu.SMEM)]
        + [vmem] * (1 + len(table) + len(chunks)),
        out_specs=vmem,
        scratch_shapes=[
            pltpu.VMEM((sum(piece.shape[0] for piece in table), width, lanes), jnp.bfloat16)
        ],
        compiler_params=pltpu.CompilerParams(vmem_limit_bytes=24 * 1024 * 1024),
        cost_estimate=pl.CostEstimate(
            flops=4 * rows * width * lanes * lanes * count,
            bytes_accessed=8 * 1024 * 1024,
            transcendentals=0,
        ),
    )(index, mask, *table, *chunks)


def shards(density, columns):
    local_rows, width, lanes = density.shape
    group = lanes // width
    total, stored = columns.shape

    jobs = np.zeros((PANELS * GROUPS, 2 + GROUPS), np.int32)
    for job in JOBS:
        jobs[place(*job)] = [*job, *arrival(*job)]
    here = lax.axis_index("row") * GROUPS + lax.axis_index("col")
    job = lax.dynamic_index_in_dim(jnp.array(jobs), here, 0, keepdims=False)
    part = lax.ppermute(density, AXES, route(start, between))
    own = lax.dynamic_slice_in_dim(columns, job[0] * local_rows, local_rows, 0)
    part, own, job = lax.optimization_barrier((part, own, job))
    part = send(part, between)
    panel, mine, order = job[0], job[1], job[2:]

    base = panel * local_rows
    goal = lax.dynamic_slice_in_dim(own, mine * group, group, 1)
    own = jnp.take(own.reshape(local_rows, GROUPS, group), order, axis=1)
    own = own.reshape(local_rows, stored)
    distance = jnp.mod(own - base + total // 2, total) - total // 2
    owner = jnp.floor_divide(distance, local_rows)
    index = table_panel(owner, panel) * local_rows + distance - owner * local_rows
    index = index.reshape(-1)
    held = lax.dynamic_slice_in_dim(columns, mine * group, group, 1)
    held = jnp.take(held, own.reshape(-1), axis=0).reshape(local_rows, stored, group)
    lane_slot = jnp.arange(lanes, dtype=jnp.int32) // width
    found = jnp.where(lane_slot == 0, held[..., :1], held[..., 1:])
    direct = jnp.where(lane_slot == 0, goal[:, None, :1], goal[:, None, 1:])
    swapped = jnp.where(lane_slot == 0, goal[:, None, 1:], goal[:, None, :1])
    mask = jnp.concatenate([found == direct, found == swapped], axis=-1)
    mask = mask.astype(jnp.float32).reshape(local_rows * stored, 2 * lanes)

    part, index, mask = lax.optimization_barrier((part, index, mask))

    one, two, three = gather_column(part)
    pair = jnp.concatenate([two, three], axis=0)
    outer, rest = pass_rows(pair, one)
    near = gather_ring(part, X_RINGS)
    near, outer, rest = lax.optimization_barrier((near, outer, rest))
    left = gather_row(near)
    table = [part, one, pair, outer, rest]
    square = product(index, mask, table, left, local_rows, False)
    left = gather_row(gather_ring(square, X_RINGS))
    result = product(index, mask, table, left + [square], local_rows, True)
    return lax.ppermute(result, AXES, route(place, start)).astype(jnp.float32)


def solution(mesh):
    placed = (P("row", None, "col"), P())
    return jax.shard_map(
        shards, mesh=mesh, in_specs=placed, out_specs=P("row", None, "col"), check_vma=False
    )
```

```python
import jax
import jax.numpy as jnp
import numpy as np
from jax import lax
from jax.experimental import pallas as pl
from jax.experimental.pallas import tpu as pltpu
from jax.sharding import PartitionSpec as P

AXES = ("row", "col")
PIECES = 5
PANELS = 64
GROUPS = 8
SPOTS = (
    (2, 3, 0, 1), (1, 0, 3, 2), (3, 0, 1, 2), (1, 2, 3, 0),
    (2, 1, 0, 3), (3, 1, 2, 0), (0, 2, 1, 3), (0, 3, 2, 1),
)


def device(half, x, y, core, z):
    return (((half * 4 + x) * 4 + y) * 2 + core) * GROUPS + z


def spot(panel, group):
    return SPOTS[group][panel // 8 % 4]


def held_at(panel, x):
    return [group for group in range(GROUPS) if spot(panel, group) == x % 4]


def lane(panel, group):
    return held_at(panel, spot(panel, group)).index(group)


def start(panel, group):
    return panel * GROUPS + group


def between(panel, group):
    return device(panel // 32, spot(panel, group), panel % 4, panel // 4 % 2, group)


def place(panel, group):
    x = spot(panel, group)
    return device(panel // 32, x, panel % 4, lane(panel, group), panel // 4 % 8)


JOBS = [(panel, group) for panel in range(PANELS) for group in range(GROUPS)]


def route(source, target):
    return sorted((source(*job), target(*job)) for job in JOBS)


def opposite(panel, group):
    return held_at(panel, spot(panel, group))[1 - lane(panel, group)]


def arrival(panel, group):
    mine = lane(panel, group)
    return [held_at(panel, x)[core] for core in (mine, 1 - mine) for x in range(4)]


def send(value, source):
    return lax.ppermute(value, AXES, route(source, place))


def gather_ring(part, ring):
    copies = jnp.concatenate([part] * 4, axis=0)
    return lax.all_to_all(copies, "row", 0, 0, tiled=True, axis_index_groups=ring)


X_RINGS = [
    [device(half, x, y, core, 0) // GROUPS for x in range(4)]
    for half in range(2) for y in range(4) for core in range(2)
]
def gather_row(near):
    return [near, send(near, lambda p, g: place(p, opposite(p, g)))]


def gather_column(part):
    return [
        send(part, lambda p, g: place(p // 4 * 4 + (p % 4 ^ flip), g))
        for flip in (1, 2, 3)
    ]


def pass_rows(pair, rest):
    pair = send(pair, lambda p, g: place((p + (-4 if p % 4 < 2 else 4)) % PANELS, g))
    rest = send(rest, lambda p, g: place((p + (4 if p % 2 else -4)) % PANELS, g))
    return pair, rest


def table_panel(owner, panel):
    y = panel % 4
    place_y = y + owner
    inner = jnp.mod(place_y, 4)
    flip = jnp.bitwise_xor(inner, y)
    return jnp.where(place_y == inner, flip, jnp.where(flip == 1, 6, flip + 2))


def product_kernel(count, group, keep, index_ref, mask_ref, *refs):
    out_ref, table_ref = refs[-2:]
    rows, width, lanes = out_ref.shape
    filled = 0
    for ref in refs[:PIECES]:
        table_ref[pl.ds(filled, ref.shape[0])] = ref[...]
        filled += ref.shape[0]
    refs = refs[PIECES:]
    chunks = [
        ref.at[pl.ds(j * rows, rows)]
        for ref in refs[:2]
        for j in range(ref.shape[0] // rows)
    ]
    blocks = count * group
    for i in range(rows):
        total = None
        for step in range(0, count, 2):
            left = jnp.concatenate([chunks[step][i], chunks[step + 1][i]], axis=1)
            pieces = []
            for b in range(step * group, (step + 2) * group):
                piece = table_ref[index_ref[i * blocks + b]]
                piece = jnp.concatenate([piece, piece], axis=1)
                mask = mask_ref[pl.ds(i * blocks + b, 1), :].astype(piece.dtype)
                pieces.append(piece * mask)
            right = jnp.concatenate(pieces, axis=0)
            part = jnp.dot(left, right, preferred_element_type=jnp.float32)
            total = part if total is None else total + part
        value = total[:, :lanes] + pltpu.roll(total[:, lanes:], width, 1)
        if keep:
            value = 3.0 * refs[2][i].astype(jnp.float32) - 2.0 * value
        out_ref[i] = value.astype(out_ref.dtype)


def product(index, mask, table, chunks, rows, keep):
    width, lanes = chunks[0].shape[1:]
    count = sum(chunk.shape[0] for chunk in chunks[:2]) // rows
    vmem = pl.BlockSpec(memory_space=pltpu.VMEM)
    return pl.pallas_call(
        lambda *refs: product_kernel(count, lanes // width, keep, *refs),
        out_shape=jax.ShapeDtypeStruct((rows, width, lanes), jnp.bfloat16),
        in_specs=[pl.BlockSpec(memory_space=pltpu.SMEM)]
        + [vmem] * (1 + len(table) + len(chunks)),
        out_specs=vmem,
        scratch_shapes=[
            pltpu.VMEM((sum(piece.shape[0] for piece in table), width, lanes), jnp.bfloat16)
        ],
        compiler_params=pltpu.CompilerParams(vmem_limit_bytes=24 * 1024 * 1024),
        cost_estimate=pl.CostEstimate(
            flops=4 * rows * width * lanes * lanes * count,
            bytes_accessed=8 * 1024 * 1024,
            transcendentals=0,
        ),
    )(index, mask, *table, *chunks)


def shards(density, columns):
    local_rows, width, lanes = density.shape
    group = lanes // width
    total, stored = columns.shape

    jobs = np.zeros((PANELS * GROUPS, 2, GROUPS), np.int32)
    for job in JOBS:
        jobs[place(*job), 0, :2] = job
        jobs[place(*job), 1] = arrival(*job)
    here = lax.axis_index("row") * GROUPS + lax.axis_index("col")
    job = lax.dynamic_index_in_dim(jnp.array(jobs), here, 0, keepdims=False)
    part = lax.ppermute(density, AXES, route(start, between))
    own = lax.dynamic_slice_in_dim(columns, job[0, 0] * local_rows, local_rows, 0)
    part, own, job = lax.optimization_barrier((part, own, job))
    part = send(part, between)
    panel, mine, order = job[0, 0], job[0, 1], job[1]

    base = panel * local_rows
    goal = lax.dynamic_slice_in_dim(own, mine * group, group, 1)
    chosen = order[:, None] == jnp.arange(GROUPS, dtype=jnp.int32)[None, :]
    own = jnp.sum(
        jnp.where(chosen[None, :, :, None], own.reshape(local_rows, 1, GROUPS, group), 0),
        axis=2,
    ).reshape(local_rows, stored)
    distance = jnp.mod(own - base + total // 2, total) - total // 2
    owner = jnp.floor_divide(distance, local_rows)
    index = table_panel(owner, panel) * local_rows + distance - owner * local_rows
    index = index.reshape(-1)
    held = lax.dynamic_slice_in_dim(columns, mine * group, group, 1)
    held = jnp.take(held, own.reshape(-1), axis=0).reshape(local_rows, stored, group)
    lane_slot = jnp.arange(lanes, dtype=jnp.int32) // width
    found = jnp.where(lane_slot == 0, held[..., :1], held[..., 1:])
    direct = jnp.where(lane_slot == 0, goal[:, None, :1], goal[:, None, 1:])
    swapped = jnp.where(lane_slot == 0, goal[:, None, 1:], goal[:, None, :1])
    mask = jnp.concatenate([found == direct, found == swapped], axis=-1)
    mask = mask.astype(jnp.float32).reshape(local_rows * stored, 2 * lanes)

    part, index, mask = lax.optimization_barrier((part, index, mask))

    one, two, three = gather_column(part)
    pair = jnp.concatenate([two, three], axis=0)
    outer, rest = pass_rows(pair, one)
    near = gather_ring(part, X_RINGS)
    near, outer, rest = lax.optimization_barrier((near, outer, rest))
    left = gather_row(near)
    table = [part, one, pair, outer, rest]
    square = product(index, mask, table, left, local_rows, False)
    left = gather_row(gather_ring(square, X_RINGS))
    result = product(index, mask, table, left + [square], local_rows, True)
    return lax.ppermute(result, AXES, route(place, start)).astype(jnp.float32)


def solution(mesh):
    placed = (P("row", None, "col"), P())
    return jax.shard_map(
        shards, mesh=mesh, in_specs=placed, out_specs=P("row", None, "col"), check_vma=False
    )
```

```python
import jax
import jax.numpy as jnp
import numpy as np
from jax import lax
from jax.experimental import pallas as pl
from jax.experimental.pallas import tpu as pltpu
from jax.sharding import PartitionSpec as P

AXES = ("row", "col")
PIECES = 5
PANELS = 64
GROUPS = 8
SPOTS = (
    (2, 3, 0, 1), (1, 0, 3, 2), (3, 0, 1, 2), (1, 2, 3, 0),
    (2, 1, 0, 3), (3, 1, 2, 0), (0, 2, 1, 3), (0, 3, 2, 1),
)


def device(half, x, y, core, z):
    return (((half * 4 + x) * 4 + y) * 2 + core) * GROUPS + z


def spot(panel, group):
    return SPOTS[group][panel // 8 % 4]


def held_at(panel, x):
    return [group for group in range(GROUPS) if spot(panel, group) == x % 4]


def lane(panel, group):
    return held_at(panel, spot(panel, group)).index(group)


def start(panel, group):
    return panel * GROUPS + group


def between(panel, group):
    return device(panel // 32, spot(panel, group), panel % 4, panel // 4 % 2, group)


def place(panel, group):
    x = spot(panel, group)
    return device(panel // 32, x, panel % 4, lane(panel, group), panel // 4 % 8)


JOBS = [(panel, group) for panel in range(PANELS) for group in range(GROUPS)]


def route(source, target):
    return sorted((source(*job), target(*job)) for job in JOBS)


def opposite(panel, group):
    return held_at(panel, spot(panel, group))[1 - lane(panel, group)]


def arrival(panel, group):
    mine = lane(panel, group)
    return [held_at(panel, x)[core] for core in (mine, 1 - mine) for x in range(4)]


def send(value, source):
    return lax.ppermute(value, AXES, route(source, place))


def gather_ring(part, ring):
    copies = jnp.concatenate([part] * 4, axis=0)
    return lax.all_to_all(copies, "row", 0, 0, tiled=True, axis_index_groups=ring)


X_RINGS = [
    [device(half, x, y, core, 0) // GROUPS for x in range(4)]
    for half in range(2) for y in range(4) for core in range(2)
]
def gather_row(near):
    return [near, send(near, lambda p, g: place(p, opposite(p, g)))]


def gather_column(part):
    return [
        send(part, lambda p, g: place(p // 4 * 4 + (p % 4 ^ flip), g))
        for flip in (1, 2, 3)
    ]


def pass_rows(part, pair):
    pair = send(pair, lambda p, g: place((p + (-4 if p % 4 < 2 else 4)) % PANELS, g))
    rest = send(part, lambda p, g: place(((p ^ 1) + (4 if p % 2 else -4)) % PANELS, g))
    return pair, rest


def table_panel(owner, panel):
    y = panel % 4
    place_y = y + owner
    inner = jnp.mod(place_y, 4)
    flip = jnp.bitwise_xor(inner, y)
    return jnp.where(place_y == inner, flip, jnp.where(flip == 1, 6, flip + 2))


def product_kernel(count, group, keep, index_ref, mask_ref, *refs):
    out_ref, table_ref = refs[-2:]
    rows, width, lanes = out_ref.shape
    filled = 0
    for ref in refs[:PIECES]:
        table_ref[pl.ds(filled, ref.shape[0])] = ref[...]
        filled += ref.shape[0]
    refs = refs[PIECES:]
    chunks = [
        ref.at[pl.ds(j * rows, rows)]
        for ref in refs[:2]
        for j in range(ref.shape[0] // rows)
    ]
    blocks = count * group
    for i in range(rows):
        total = None
        for step in range(0, count, 2):
            left = jnp.concatenate([chunks[step][i], chunks[step + 1][i]], axis=1)
            pieces = []
            for b in range(step * group, (step + 2) * group):
                piece = table_ref[index_ref[i * blocks + b]]
                piece = jnp.concatenate([piece, piece], axis=1)
                mask = mask_ref[pl.ds(i * blocks + b, 1), :].astype(piece.dtype)
                pieces.append(piece * mask)
            right = jnp.concatenate(pieces, axis=0)
            part = jnp.dot(left, right, preferred_element_type=jnp.float32)
            total = part if total is None else total + part
        value = total[:, :lanes] + pltpu.roll(total[:, lanes:], width, 1)
        if keep:
            value = 3.0 * refs[2][i].astype(jnp.float32) - 2.0 * value
        out_ref[i] = value.astype(out_ref.dtype)


def product(index, mask, table, chunks, rows, keep):
    width, lanes = chunks[0].shape[1:]
    count = sum(chunk.shape[0] for chunk in chunks[:2]) // rows
    vmem = pl.BlockSpec(memory_space=pltpu.VMEM)
    return pl.pallas_call(
        lambda *refs: product_kernel(count, lanes // width, keep, *refs),
        out_shape=jax.ShapeDtypeStruct((rows, width, lanes), jnp.bfloat16),
        in_specs=[pl.BlockSpec(memory_space=pltpu.SMEM)]
        + [vmem] * (1 + len(table) + len(chunks)),
        out_specs=vmem,
        scratch_shapes=[
            pltpu.VMEM((sum(piece.shape[0] for piece in table), width, lanes), jnp.bfloat16)
        ],
        compiler_params=pltpu.CompilerParams(vmem_limit_bytes=24 * 1024 * 1024),
        cost_estimate=pl.CostEstimate(
            flops=4 * rows * width * lanes * lanes * count,
            bytes_accessed=8 * 1024 * 1024,
            transcendentals=0,
        ),
    )(index, mask, *table, *chunks)


def shards(density, columns):
    local_rows, width, lanes = density.shape
    group = lanes // width
    total, stored = columns.shape

    jobs = np.zeros((PANELS * GROUPS, 2, GROUPS), np.int32)
    for job in JOBS:
        jobs[place(*job), 0, :2] = job
        jobs[place(*job), 1] = arrival(*job)
    here = lax.axis_index("row") * GROUPS + lax.axis_index("col")
    job = lax.dynamic_index_in_dim(jnp.array(jobs), here, 0, keepdims=False)
    part = lax.ppermute(density, AXES, route(start, between))
    own = lax.dynamic_slice_in_dim(columns, job[0, 0] * local_rows, local_rows, 0)
    part, own, job = lax.optimization_barrier((part, own, job))
    part = send(part, between)
    panel, mine, order = job[0, 0], job[0, 1], job[1]

    base = panel * local_rows
    goal = lax.dynamic_slice_in_dim(own, mine * group, group, 1)
    chosen = order[:, None] == jnp.arange(GROUPS, dtype=jnp.int32)[None, :]
    own = jnp.sum(
        jnp.where(chosen[None, :, :, None], own.reshape(local_rows, 1, GROUPS, group), 0),
        axis=2,
    ).reshape(local_rows, stored)
    distance = jnp.mod(own - base + total // 2, total) - total // 2
    owner = jnp.floor_divide(distance, local_rows)
    index = table_panel(owner, panel) * local_rows + distance - owner * local_rows
    index = index.reshape(-1)
    held = lax.dynamic_slice_in_dim(columns, mine * group, group, 1)
    held = jnp.take(held, own.reshape(-1), axis=0).reshape(local_rows, stored, group)
    lane_slot = jnp.arange(lanes, dtype=jnp.int32) // width
    found = jnp.where(lane_slot == 0, held[..., :1], held[..., 1:])
    direct = jnp.where(lane_slot == 0, goal[:, None, :1], goal[:, None, 1:])
    swapped = jnp.where(lane_slot == 0, goal[:, None, 1:], goal[:, None, :1])
    mask = jnp.concatenate([found == direct, found == swapped], axis=-1)
    mask = mask.astype(jnp.float32).reshape(local_rows * stored, 2 * lanes)

    part, index, mask = lax.optimization_barrier((part, index, mask))

    one, two, three = gather_column(part)
    pair = jnp.concatenate([two, three], axis=0)
    outer, rest = pass_rows(part, pair)
    near = gather_ring(part, X_RINGS)
    near, outer, rest, one = lax.optimization_barrier((near, outer, rest, one))
    left = gather_row(near)
    table = [part, one, pair, outer, rest]
    square = product(index, mask, table, left, local_rows, False)
    left = gather_row(gather_ring(square, X_RINGS))
    result = product(index, mask, table, left + [square], local_rows, True)
    return lax.ppermute(result, AXES, route(place, start)).astype(jnp.float32)


def solution(mesh):
    placed = (P("row", None, "col"), P())
    return jax.shard_map(
        shards, mesh=mesh, in_specs=placed, out_specs=P("row", None, "col"), check_vma=False
    )
```

```python
import jax
import jax.numpy as jnp
import numpy as np
from jax import lax
from jax.experimental import pallas as pl
from jax.experimental.pallas import tpu as pltpu
from jax.sharding import PartitionSpec as P

AXES = ("row", "col")
PIECES = 5
PANELS = 64
GROUPS = 8
SPOTS = (
    (2, 3, 0, 1), (1, 0, 3, 2), (3, 0, 1, 2), (1, 2, 3, 0),
    (2, 1, 0, 3), (3, 1, 2, 0), (0, 2, 1, 3), (0, 3, 2, 1),
)


def device(half, x, y, core, z):
    return (((half * 4 + x) * 4 + y) * 2 + core) * GROUPS + z


def spot(panel, group):
    return SPOTS[group][panel // 8 % 4]


def held_at(panel, x):
    return [group for group in range(GROUPS) if spot(panel, group) == x % 4]


def lane(panel, group):
    return held_at(panel, spot(panel, group)).index(group)


def start(panel, group):
    return panel * GROUPS + group


def between(panel, group):
    return device(panel // 32, spot(panel, group), panel % 4, panel // 4 % 2, group)


def place(panel, group):
    x = spot(panel, group)
    return device(panel // 32, x, panel % 4, lane(panel, group), panel // 4 % 8)


JOBS = [(panel, group) for panel in range(PANELS) for group in range(GROUPS)]


def route(source, target):
    return sorted((source(*job), target(*job)) for job in JOBS)


def opposite(panel, group):
    return held_at(panel, spot(panel, group))[1 - lane(panel, group)]


def plane_order(panel):
    return [group for x in range(4) for group in held_at(panel, x)]


def arrival(panel, group):
    mine = lane(panel, group)
    return [held_at(panel, x)[core] for core in (mine, 1 - mine) for x in range(4)]


def send(value, source):
    return lax.ppermute(value, AXES, route(source, place))


def gather_ring(part, ring):
    copies = jnp.concatenate([part] * 4, axis=0)
    return lax.all_to_all(copies, "row", 0, 0, tiled=True, axis_index_groups=ring)


X_RINGS = [
    [device(half, x, y, core, 0) // GROUPS for x in range(4)]
    for half in range(2) for y in range(4) for core in range(2)
]
CORES = [[2 * chip, 2 * chip + 1] for chip in range(PANELS // 2)]


def gather_cores(near, rows):
    return [
        lax.all_gather(
            near[j : j + rows], "row", axis=0, tiled=True, axis_index_groups=CORES
        )
        for j in range(0, near.shape[0], rows)
    ]


def gather_row(near):
    return [near, send(near, lambda p, g: place(p, opposite(p, g)))]


def gather_column(part):
    return [
        send(part, lambda p, g: place(p // 4 * 4 + (p % 4 ^ flip), g))
        for flip in (1, 2, 3)
    ]


def pass_rows(part, pair):
    pair = send(pair, lambda p, g: place((p + (-4 if p % 4 < 2 else 4)) % PANELS, g))
    rest = send(part, lambda p, g: place(((p ^ 1) + (4 if p % 2 else -4)) % PANELS, g))
    return pair, rest


def table_panel(owner, panel):
    y = panel % 4
    place_y = y + owner
    inner = jnp.mod(place_y, 4)
    flip = jnp.bitwise_xor(inner, y)
    return jnp.where(place_y == inner, flip, jnp.where(flip == 1, 6, flip + 2))


def product_kernel(operands, count, group, keep, index_ref, mask_ref, *refs):
    out_ref, table_ref = refs[-2:]
    rows, width, lanes = out_ref.shape
    filled = 0
    for ref in refs[:PIECES]:
        table_ref[pl.ds(filled, ref.shape[0])] = ref[...]
        filled += ref.shape[0]
    refs = refs[PIECES:]
    chunks = [
        ref.at[pl.ds(j * rows, rows)]
        for ref in refs[:operands]
        for j in range(ref.shape[0] // rows)
    ]
    blocks = count * group
    for i in range(rows):
        total = None
        for step in range(0, count, 2):
            left = jnp.concatenate([chunks[step][i], chunks[step + 1][i]], axis=1)
            pieces = []
            for b in range(step * group, (step + 2) * group):
                piece = table_ref[index_ref[i * blocks + b]]
                piece = jnp.concatenate([piece, piece], axis=1)
                mask = mask_ref[pl.ds(i * blocks + b, 1), :].astype(piece.dtype)
                pieces.append(piece * mask)
            right = jnp.concatenate(pieces, axis=0)
            part = jnp.dot(left, right, preferred_element_type=jnp.float32)
            total = part if total is None else total + part
        value = total[:, :lanes] + pltpu.roll(total[:, lanes:], width, 1)
        if keep:
            value = 3.0 * refs[operands][i].astype(jnp.float32) - 2.0 * value
        out_ref[i] = value.astype(out_ref.dtype)


def product(index, mask, table, chunks, rows, kept=()):
    width, lanes = chunks[0].shape[1:]
    count = sum(chunk.shape[0] for chunk in chunks) // rows
    vmem = pl.BlockSpec(memory_space=pltpu.VMEM)
    return pl.pallas_call(
        lambda *refs: product_kernel(
            len(chunks), count, lanes // width, bool(kept), *refs
        ),
        out_shape=jax.ShapeDtypeStruct((rows, width, lanes), jnp.bfloat16),
        in_specs=[pl.BlockSpec(memory_space=pltpu.SMEM)]
        + [vmem] * (1 + len(table) + len(chunks) + len(kept)),
        out_specs=vmem,
        scratch_shapes=[
            pltpu.VMEM((sum(piece.shape[0] for piece in table), width, lanes), jnp.bfloat16)
        ],
        compiler_params=pltpu.CompilerParams(vmem_limit_bytes=24 * 1024 * 1024),
        cost_estimate=pl.CostEstimate(
            flops=4 * rows * width * lanes * lanes * count,
            bytes_accessed=8 * 1024 * 1024,
            transcendentals=0,
        ),
    )(index, mask, *table, *chunks, *kept)


def shards(density, columns):
    local_rows, width, lanes = density.shape
    group = lanes // width
    total, stored = columns.shape

    jobs = np.zeros((PANELS * GROUPS, 2 + 2 * GROUPS), np.int32)
    for job in JOBS:
        jobs[place(*job)] = [*job, *plane_order(job[0]), *arrival(*job)]
    here = lax.axis_index("row") * GROUPS + lax.axis_index("col")
    job = lax.dynamic_index_in_dim(jnp.array(jobs), here, 0, keepdims=False)
    part = lax.ppermute(density, AXES, route(start, between))
    own = lax.dynamic_slice_in_dim(columns, job[0] * local_rows, local_rows, 0)
    part, own, job = lax.optimization_barrier((part, own, job))
    part = send(part, between)
    panel, mine, order = job[0], job[1], job[2:]

    base = panel * local_rows
    goal = lax.dynamic_slice_in_dim(own, mine * group, group, 1)
    orders = order.reshape(2, GROUPS)
    own = jnp.take(own.reshape(local_rows, GROUPS, group), orders, axis=1)
    own = own.swapaxes(0, 1).reshape(2, local_rows, stored)
    distance = jnp.mod(own - base + total // 2, total) - total // 2
    owner = jnp.floor_divide(distance, local_rows)
    index = table_panel(owner, panel) * local_rows + distance - owner * local_rows
    index = index.reshape(2, -1)
    held = lax.dynamic_slice_in_dim(columns, mine * group, group, 1)
    held = jnp.take(held, own.reshape(-1), axis=0).reshape(2, local_rows, stored, group)
    lane_slot = jnp.arange(lanes, dtype=jnp.int32) // width
    found = jnp.where(lane_slot == 0, held[..., :1], held[..., 1:])
    direct = jnp.where(lane_slot == 0, goal[:, None, :1], goal[:, None, 1:])
    swapped = jnp.where(lane_slot == 0, goal[:, None, 1:], goal[:, None, :1])
    mask = jnp.concatenate([found == direct, found == swapped], axis=-1)
    mask = mask.astype(jnp.float32).reshape(2, local_rows * stored, 2 * lanes)
    part, index, mask = lax.optimization_barrier((part, index, mask))

    one, two, three = gather_column(part)
    pair = jnp.concatenate([two, three], axis=0)
    outer, rest = pass_rows(part, pair)
    near = gather_ring(part, X_RINGS)
    left = gather_cores(near, local_rows)
    table = [part, one, pair, outer, rest]
    square = product(index[0], mask[0], table, left, local_rows)
    left = gather_row(gather_ring(square, X_RINGS))
    result = product(index[1], mask[1], table, left, local_rows, [square])
    return lax.ppermute(result, AXES, route(place, start)).astype(jnp.float32)


def solution(mesh):
    placed = (P("row", None, "col"), P())
    return jax.shard_map(
        shards, mesh=mesh, in_specs=placed, out_specs=P("row", None, "col"), check_vma=False
    )
```

```python
import jax
import jax.numpy as jnp
import numpy as np
from jax import lax
from jax.experimental import pallas as pl
from jax.experimental.pallas import tpu as pltpu
from jax.sharding import PartitionSpec as P

AXES = ("row", "col")
PIECES = 5
PANELS = 64
GROUPS = 8
SPOTS = (
    (2, 3, 0, 1), (1, 0, 3, 2), (3, 0, 1, 2), (1, 2, 3, 0),
    (2, 1, 0, 3), (3, 1, 2, 0), (0, 2, 1, 3), (0, 3, 2, 1),
)


def device(half, x, y, core, z):
    return (((half * 4 + x) * 4 + y) * 2 + core) * GROUPS + z


def spot(panel, group):
    return SPOTS[group][panel // 8 % 4]


def held_at(panel, x):
    return [group for group in range(GROUPS) if spot(panel, group) == x % 4]


def lane(panel, group):
    return held_at(panel, spot(panel, group)).index(group)


def start(panel, group):
    return panel * GROUPS + group


def between(panel, group):
    return device(panel // 32, spot(panel, group), panel % 4, panel // 4 % 2, group)


def place(panel, group):
    x = spot(panel, group)
    return device(panel // 32, x, panel % 4, lane(panel, group), panel // 4 % 8)


JOBS = [(panel, group) for panel in range(PANELS) for group in range(GROUPS)]


def route(source, target):
    return sorted((source(*job), target(*job)) for job in JOBS)


def opposite(panel, group):
    return held_at(panel, spot(panel, group))[1 - lane(panel, group)]


def across(panel, group, flip):
    return held_at(panel, spot(panel, group) ^ flip)[lane(panel, group)]


def near_first(panel, group):
    near = [across(panel, group, flip) for flip in range(4)]
    return near + [opposite(panel, other) for other in near]


def arrival(panel, group):
    mine = lane(panel, group)
    return [held_at(panel, x)[core] for core in (mine, 1 - mine) for x in range(4)]


def send(value, source):
    return lax.ppermute(value, AXES, route(source, place))


def gather_ring(part, ring):
    copies = jnp.concatenate([part] * 4, axis=0)
    return lax.all_to_all(copies, "row", 0, 0, tiled=True, axis_index_groups=ring)


X_RINGS = [
    [device(half, x, y, core, 0) // GROUPS for x in range(4)]
    for half in range(2) for y in range(4) for core in range(2)
]
def gather_square(square):
    near = [
        send(square, lambda p, g: place(p, across(p, g, flip))) for flip in (1, 2, 3)
    ]
    near = jnp.concatenate(near, axis=0)
    far = [send(piece, lambda p, g: place(p, opposite(p, g))) for piece in (square, near)]
    return [square, near] + far


def gather_row(near):
    return [near, send(near, lambda p, g: place(p, opposite(p, g)))]


def gather_column(part):
    return [
        send(part, lambda p, g: place(p // 4 * 4 + (p % 4 ^ flip), g))
        for flip in (1, 2, 3)
    ]


def pass_rows(pair, rest):
    pair = send(pair, lambda p, g: place((p + (-4 if p % 4 < 2 else 4)) % PANELS, g))
    rest = send(rest, lambda p, g: place((p + (4 if p % 2 else -4)) % PANELS, g))
    return pair, rest


def table_panel(owner, panel):
    y = panel % 4
    place_y = y + owner
    inner = jnp.mod(place_y, 4)
    flip = jnp.bitwise_xor(inner, y)
    return jnp.where(place_y == inner, flip, jnp.where(flip == 1, 6, flip + 2))


def product_kernel(operands, count, group, keep, index_ref, mask_ref, *refs):
    out_ref, table_ref = refs[-2:]
    rows, width, lanes = out_ref.shape
    filled = 0
    for ref in refs[:PIECES]:
        table_ref[pl.ds(filled, ref.shape[0])] = ref[...]
        filled += ref.shape[0]
    refs = refs[PIECES:]
    chunks = [
        ref.at[pl.ds(j * rows, rows)]
        for ref in refs[:operands]
        for j in range(ref.shape[0] // rows)
    ]
    blocks = count * group
    for i in range(rows):
        total = None
        for step in range(0, count, 2):
            left = jnp.concatenate([chunks[step][i], chunks[step + 1][i]], axis=1)
            pieces = []
            for b in range(step * group, (step + 2) * group):
                piece = table_ref[index_ref[i * blocks + b]]
                piece = jnp.concatenate([piece, piece], axis=1)
                mask = mask_ref[pl.ds(i * blocks + b, 1), :].astype(piece.dtype)
                pieces.append(piece * mask)
            right = jnp.concatenate(pieces, axis=0)
            part = jnp.dot(left, right, preferred_element_type=jnp.float32)
            total = part if total is None else total + part
        value = total[:, :lanes] + pltpu.roll(total[:, lanes:], width, 1)
        if keep:
            value = 3.0 * refs[operands][i].astype(jnp.float32) - 2.0 * value
        out_ref[i] = value.astype(out_ref.dtype)


def product(index, mask, table, chunks, rows, kept=()):
    width, lanes = chunks[0].shape[1:]
    count = sum(chunk.shape[0] for chunk in chunks) // rows
    vmem = pl.BlockSpec(memory_space=pltpu.VMEM)
    return pl.pallas_call(
        lambda *refs: product_kernel(
            len(chunks), count, lanes // width, bool(kept), *refs
        ),
        out_shape=jax.ShapeDtypeStruct((rows, width, lanes), jnp.bfloat16),
        in_specs=[pl.BlockSpec(memory_space=pltpu.SMEM)]
        + [vmem] * (1 + len(table) + len(chunks) + len(kept)),
        out_specs=vmem,
        scratch_shapes=[
            pltpu.VMEM((sum(piece.shape[0] for piece in table), width, lanes), jnp.bfloat16)
        ],
        compiler_params=pltpu.CompilerParams(vmem_limit_bytes=24 * 1024 * 1024),
        cost_estimate=pl.CostEstimate(
            flops=4 * rows * width * lanes * lanes * count,
            bytes_accessed=8 * 1024 * 1024,
            transcendentals=0,
        ),
    )(index, mask, *table, *chunks, *kept)


def shards(density, columns):
    local_rows, width, lanes = density.shape
    group = lanes // width
    total, stored = columns.shape

    jobs = np.zeros((PANELS * GROUPS, 2 + 2 * GROUPS), np.int32)
    for job in JOBS:
        jobs[place(*job)] = [*job, *arrival(*job), *near_first(*job)]
    here = lax.axis_index("row") * GROUPS + lax.axis_index("col")
    job = lax.dynamic_index_in_dim(jnp.array(jobs), here, 0, keepdims=False)
    part = lax.ppermute(density, AXES, route(start, between))
    own = lax.dynamic_slice_in_dim(columns, job[0] * local_rows, local_rows, 0)
    part, own, job = lax.optimization_barrier((part, own, job))
    part = send(part, between)
    panel, mine, order = job[0], job[1], job[2:]

    base = panel * local_rows
    goal = lax.dynamic_slice_in_dim(own, mine * group, group, 1)
    orders = order.reshape(2, GROUPS)
    own = jnp.take(own.reshape(local_rows, GROUPS, group), orders, axis=1)
    own = own.swapaxes(0, 1).reshape(2, local_rows, stored)
    distance = jnp.mod(own - base + total // 2, total) - total // 2
    owner = jnp.floor_divide(distance, local_rows)
    index = table_panel(owner, panel) * local_rows + distance - owner * local_rows
    index = index.reshape(2, -1)
    held = lax.dynamic_slice_in_dim(columns, mine * group, group, 1)
    held = jnp.take(held, own.reshape(-1), axis=0).reshape(2, local_rows, stored, group)
    lane_slot = jnp.arange(lanes, dtype=jnp.int32) // width
    found = jnp.where(lane_slot == 0, held[..., :1], held[..., 1:])
    direct = jnp.where(lane_slot == 0, goal[:, None, :1], goal[:, None, 1:])
    swapped = jnp.where(lane_slot == 0, goal[:, None, 1:], goal[:, None, :1])
    mask = jnp.concatenate([found == direct, found == swapped], axis=-1)
    mask = mask.astype(jnp.float32).reshape(2, local_rows * stored, 2 * lanes)
    part, index, mask = lax.optimization_barrier((part, index, mask))

    one, two, three = gather_column(part)
    pair = jnp.concatenate([two, three], axis=0)
    outer, rest = pass_rows(pair, one)
    near = gather_ring(part, X_RINGS)
    near, outer, rest = lax.optimization_barrier((near, outer, rest))
    left = gather_row(near)
    table = [part, one, pair, outer, rest]
    square = product(index[0], mask[0], table, left, local_rows)
    left = gather_square(square)
    result = product(index[1], mask[1], table, left, local_rows, [square])
    return lax.ppermute(result, AXES, route(place, start)).astype(jnp.float32)


def solution(mesh):
    placed = (P("row", None, "col"), P())
    return jax.shard_map(
        shards, mesh=mesh, in_specs=placed, out_specs=P("row", None, "col"), check_vma=False
    )
```

```python
import jax
import jax.numpy as jnp
import numpy as np
from jax import lax
from jax.experimental import pallas as pl
from jax.experimental.pallas import tpu as pltpu
from jax.sharding import PartitionSpec as P

AXES = ("row", "col")
PIECES = 5
PANELS = 64
GROUPS = 8
SPOTS = (
    (2, 3, 0, 1), (1, 0, 3, 2), (3, 0, 1, 2), (1, 2, 3, 0),
    (2, 1, 0, 3), (3, 1, 2, 0), (0, 2, 1, 3), (0, 3, 2, 1),
)


def device(half, x, y, core, z):
    return (((half * 4 + x) * 4 + y) * 2 + core) * GROUPS + z


def spot(panel, group):
    return SPOTS[group][panel // 8 % 4]


def held_at(panel, x):
    return [group for group in range(GROUPS) if spot(panel, group) == x % 4]


def lane(panel, group):
    return held_at(panel, spot(panel, group)).index(group)


def start(panel, group):
    return panel * GROUPS + group


def between(panel, group):
    return device(panel // 32, spot(panel, group), panel % 4, panel // 4 % 2, group)


def place(panel, group):
    x = spot(panel, group)
    return device(panel // 32, x, panel % 4, lane(panel, group), panel // 4 % 8)


JOBS = [(panel, group) for panel in range(PANELS) for group in range(GROUPS)]


def route(source, target):
    return sorted((source(*job), target(*job)) for job in JOBS)


def opposite(panel, group):
    return held_at(panel, spot(panel, group))[1 - lane(panel, group)]


def arrival(panel, group):
    mine = lane(panel, group)
    return [held_at(panel, x)[core] for core in (mine, 1 - mine) for x in range(4)]


def send(value, source):
    return lax.ppermute(value, AXES, route(source, place))


def gather_ring(part, ring):
    copies = jnp.concatenate([part] * 4, axis=0)
    return lax.all_to_all(copies, "row", 0, 0, tiled=True, axis_index_groups=ring)


X_RINGS = [
    [device(half, x, y, core, 0) // GROUPS for x in range(4)]
    for half in range(2) for y in range(4) for core in range(2)
]
def gather_row(near):
    return [near, send(near, lambda p, g: place(p, opposite(p, g)))]


def gather_column(part):
    return [
        send(part, lambda p, g: place(p // 4 * 4 + (p % 4 ^ flip), g))
        for flip in (1, 2, 3)
    ]


def pass_rows(pair, rest):
    pair = send(pair, lambda p, g: place((p + (-4 if p % 4 < 2 else 4)) % PANELS, g))
    rest = send(rest, lambda p, g: place((p + (4 if p % 2 else -4)) % PANELS, g))
    return pair, rest


def table_panel(owner, panel):
    y = panel % 4
    place_y = y + owner
    inner = jnp.mod(place_y, 4)
    flip = jnp.bitwise_xor(inner, y)
    return jnp.where(place_y == inner, flip, jnp.where(flip == 1, 6, flip + 2))


def product_kernel(count, group, keep, index_ref, mask_ref, *refs):
    out_ref, table_ref = refs[-2:]
    rows, width, lanes = out_ref.shape
    filled = 0
    for ref in refs[:PIECES]:
        table_ref[pl.ds(filled, ref.shape[0])] = ref[...]
        filled += ref.shape[0]
    refs = refs[PIECES:]
    chunks = [
        ref.at[pl.ds(j * rows, rows)]
        for ref in refs[:2]
        for j in range(ref.shape[0] // rows)
    ]
    blocks = count * group
    for i in range(rows):
        total = None
        for step in range(0, count, 2):
            left = jnp.concatenate([chunks[step][i], chunks[step + 1][i]], axis=1)
            pieces = []
            for b in range(step * group, (step + 2) * group):
                piece = table_ref[index_ref[i * blocks + b]]
                piece = jnp.concatenate([piece, piece], axis=1)
                mask = mask_ref[pl.ds(i * blocks + b, 1), :].astype(piece.dtype)
                pieces.append(piece * mask)
            right = jnp.concatenate(pieces, axis=0)
            part = jnp.dot(left, right, preferred_element_type=jnp.float32)
            total = part if total is None else total + part
        value = total[:, :lanes] + pltpu.roll(total[:, lanes:], width, 1)
        if keep:
            value = 3.0 * refs[2][i].astype(jnp.float32) - 2.0 * value
        out_ref[i] = value.astype(out_ref.dtype)


def product(index, mask, table, chunks, rows, keep):
    width, lanes = chunks[0].shape[1:]
    count = sum(chunk.shape[0] for chunk in chunks[:2]) // rows
    vmem = pl.BlockSpec(memory_space=pltpu.VMEM)
    return pl.pallas_call(
        lambda *refs: product_kernel(count, lanes // width, keep, *refs),
        out_shape=jax.ShapeDtypeStruct((rows, width, lanes), jnp.bfloat16),
        in_specs=[pl.BlockSpec(memory_space=pltpu.SMEM)]
        + [vmem] * (1 + len(table) + len(chunks)),
        out_specs=vmem,
        scratch_shapes=[
            pltpu.VMEM((sum(piece.shape[0] for piece in table), width, lanes), jnp.bfloat16)
        ],
        compiler_params=pltpu.CompilerParams(vmem_limit_bytes=24 * 1024 * 1024),
        cost_estimate=pl.CostEstimate(
            flops=4 * rows * width * lanes * lanes * count,
            bytes_accessed=8 * 1024 * 1024,
            transcendentals=0,
        ),
    )(index, mask, *table, *chunks)


def shards(density, columns):
    local_rows, width, lanes = density.shape
    group = lanes // width
    total, stored = columns.shape

    jobs = np.zeros((PANELS * GROUPS, 2, GROUPS), np.int32)
    for job in JOBS:
        jobs[place(*job), 0, :2] = job
        jobs[place(*job), 1] = arrival(*job)
    here = lax.axis_index("row") * GROUPS + lax.axis_index("col")
    job = lax.dynamic_index_in_dim(jnp.array(jobs), here, 0, keepdims=False)
    part = lax.ppermute(density, AXES, route(start, between))
    own = lax.dynamic_slice_in_dim(columns, job[0, 0] * local_rows, local_rows, 0)
    part, own = lax.optimization_barrier((part, own))
    part = send(part, between)
    panel, mine, order = job[0, 0], job[0, 1], job[1]

    base = panel * local_rows
    goal = lax.dynamic_slice_in_dim(own, mine * group, group, 1)
    chosen = order[:, None] == jnp.arange(GROUPS, dtype=jnp.int32)[None, :]
    own = jnp.sum(
        jnp.where(chosen[None, :, :, None], own.reshape(local_rows, 1, GROUPS, group), 0),
        axis=2,
    ).reshape(local_rows, stored)
    distance = jnp.mod(own - base + total // 2, total) - total // 2
    owner = jnp.floor_divide(distance, local_rows)
    index = table_panel(owner, panel) * local_rows + distance - owner * local_rows
    index = index.reshape(-1)
    held = lax.dynamic_slice_in_dim(columns, mine * group, group, 1)
    held = jnp.take(held, own.reshape(-1), axis=0).reshape(local_rows, stored, group)
    lane_slot = jnp.arange(lanes, dtype=jnp.int32) // width
    found = jnp.where(lane_slot == 0, held[..., :1], held[..., 1:])
    direct = jnp.where(lane_slot == 0, goal[:, None, :1], goal[:, None, 1:])
    swapped = jnp.where(lane_slot == 0, goal[:, None, 1:], goal[:, None, :1])
    mask = jnp.concatenate([found == direct, found == swapped], axis=-1)
    mask = mask.astype(jnp.float32).reshape(local_rows * stored, 2 * lanes)

    part, index, mask = lax.optimization_barrier((part, index, mask))

    one, two, three = gather_column(part)
    pair = jnp.concatenate([two, three], axis=0)
    outer, rest = pass_rows(pair, one)
    near = gather_ring(part, X_RINGS)
    near, outer, rest = lax.optimization_barrier((near, outer, rest))
    left = gather_row(near)
    table = [part, one, pair, outer, rest]
    square = product(index, mask, table, left, local_rows, False)
    left = gather_row(gather_ring(square, X_RINGS))
    result = product(index, mask, table, left + [square], local_rows, True)
    return lax.ppermute(result, AXES, route(place, start)).astype(jnp.float32)


def solution(mesh):
    placed = (P("row", None, "col"), P())
    return jax.shard_map(
        shards, mesh=mesh, in_specs=placed, out_specs=P("row", None, "col"), check_vma=False
    )
```
